128 devices in a mesh: ctx: 32 (over x_lo, z, y), tp: 4 (over x_hi, core).
Axes of the slice: x: 4 (x_hi: 2, x_lo: 2; x = x_hi * 2 + x_lo), y: 4, z: 4, core: 2. Of those that a mesh axis runs over, the one named last changes fastest.
Arguments:
- tokens: bfloat16 [8192, 768], P('ctx'), may hold values from -6 to 6
- block_order: int32 [64], replicated, may hold values from 0 to 63, each once
- cotangent: bfloat16 [8192, 768], P('ctx'), may hold values from -20 to 20
- w_qkv: bfloat16 [768, 2304], P(None, 'tp'), may hold values from -0.3125 to 0.3125
- b_qkv: float32 [2304], P('tp'), may hold values from -3 to 3
- w_dense: bfloat16 [768, 768], P('tp'), may hold values from -0.75 to 0.75
- b_dense: float32 [768], replicated, may hold values from -3 to 3
- w_up: bfloat16 [768, 3072], P(None, 'tp'), may hold values from -0.21875 to 0.21875
- b_up: float32 [3072], P('tp'), may hold values from -3 to 3
- w_down: bfloat16 [3072, 768], P('tp'), may hold values from -0.109375 to 0.109375
- b_down: float32 [768], replicated, may hold values from -3 to 3
- gain_attn: float32 [768], replicated, may hold values from 0.25 to 1.75
- shift_attn: float32 [768], replicated, may hold values from -3 to 3
- gain_mlp: float32 [768], replicated, may hold values from 0.25 to 1.75
- shift_mlp: float32 [768], replicated, may hold values from -3 to 3
Outputs:
- output: bfloat16 [8192, 768], P('ctx')
- grad_tokens: bfloat16 [8192, 768], P('ctx')
- grad_w_qkv: float32 [768, 2304], P(None, 'tp')
- grad_b_qkv: float32 [2304], P('tp')
- grad_w_dense: float32 [768, 768], P('tp')
- grad_b_dense: float32 [768], replicated
- grad_w_up: float32 [768, 3072], P(None, 'tp')
- grad_b_up: float32 [3072], P('tp')
- grad_w_down: float32 [3072, 768], P('tp')
- grad_b_down: float32 [768], replicated
- grad_gain_attn: float32 [768], replicated
- grad_shift_attn: float32 [768], replicated
- grad_gain_mlp: float32 [768], replicated
- grad_shift_mlp: float32 [768], replicated
The draws below stay inside these ranges and needn't reach their ends.
Inputs may be any that keep to these rules, and one draw needn't show every extreme that they name: A permutation: storage block s, rows s * 128 to (s + 1) * 128 - 1, holds the sequence block block_order[s].
All inputs are finite; a program needn't handle non-finite values.
Results may differ from the reference program's by a relative error of at most 0.028.
Values may be sent and summed in bfloat16 or wider, within the bound.
No kernel may reach another device: no remote copies, remote signals or barrier semaphores. Data moves between devices by JAX's collectives and lax.ppermute only.
A program may use at most 128 MiB of HBM per device.

```python
import math
import jax
import jax.numpy as jnp
from jax import lax

D = 768
HEADS = 12
HEAD = 64
ROT = 16
FF = 3072
SEQ = 8192
HALF = 128
BLOCKS = 64


def draw_cotangent(key, part):
    key = jax.random.fold_in(key, 11)
    row_index = jnp.arange(SEQ, dtype=jnp.float32)
    rising = jnp.exp(math.log(3.0) * row_index / max(SEQ - 1, 1))[:, None]
    drawn_values = jax.random.normal(key, (SEQ, D), jnp.float32) * rising
    return jnp.clip(drawn_values, -20.0, 20.0).astype(jnp.bfloat16)


def shard_levels(own_key, extent, cuts, least, top_value):
    factor_of, own = 1.0, jax.random.fold_in(own_key, 6)
    for axis_at, blocks in cuts:
        heights = jnp.exp(jax.random.uniform(jax.random.fold_in(own, axis_at), (blocks,), jnp.float32, least / len(cuts), top_value / len(cuts)))
        factor_of = factor_of * jnp.repeat(heights, extent[axis_at] // blocks).reshape([-1 if axis == axis_at else 1 for axis in range(len(extent))])
    return factor_of


def gaussian(rng, extent, width, reach, shards=(), kind=jnp.bfloat16):
    gain = shard_levels(rng, extent, shards, -0.22, 0.18) if shards else 1.0
    array = jax.random.normal(rng, extent, jnp.float32) * width * gain
    return jnp.minimum(jnp.maximum(array, -reach), reach).astype(kind)


def setup_inputs(seed: int = 0) -> dict:
    streams_of = jax.random.split(jax.random.key(seed), 16)
    tokens = gaussian(streams_of[0], (SEQ, D), 1.0, 6.0, ((0, 32),))
    block_order = jax.random.permutation(streams_of[1], BLOCKS).astype(jnp.int32)
    cotangent = draw_cotangent(jax.random.fold_in(streams_of[15], 71), 0)
    w_qkv = gaussian(streams_of[3], (D, 3 * D), (D // 2) ** -0.5, 0.3125, ((1, 4),))
    b_qkv = gaussian(streams_of[4], (3 * D,), 0.5, 3.0, ((0, 4),), jnp.float32)
    w_dense = gaussian(streams_of[5], (D, D), HEAD ** -0.5, 0.75, ((0, 4),))
    b_dense = gaussian(streams_of[6], (D,), 0.5, 3.0, (), jnp.float32)
    w_up = gaussian(streams_of[7], (D, FF), D ** -0.5, 0.21875, ((1, 4),))
    b_up = gaussian(streams_of[8], (FF,), 0.5, 3.0, ((0, 4),), jnp.float32)
    w_down = gaussian(streams_of[9], (FF, D), FF ** -0.5, 0.109375, ((0, 4),))
    b_down = gaussian(streams_of[10], (D,), 0.5, 3.0, (), jnp.float32)
    gain_attn = jnp.clip(1.0 + 0.15 * jax.random.normal(streams_of[11], (D,), jnp.float32), 0.25, 1.75)
    shift_attn = gaussian(streams_of[12], (D,), 0.3, 3.0, (), jnp.float32)
    gain_mlp = jnp.clip(1.0 + 0.15 * jax.random.normal(streams_of[13], (D,), jnp.float32), 0.25, 1.75)
    shift_mlp = gaussian(streams_of[14], (D,), 0.3, 3.0, (), jnp.float32)
    return dict(tokens=tokens, block_order=block_order, cotangent=cotangent, w_qkv=w_qkv, b_qkv=b_qkv, w_dense=w_dense, b_dense=b_dense, w_up=w_up, b_up=b_up, w_down=w_down, b_down=b_down, gain_attn=gain_attn, shift_attn=shift_attn, gain_mlp=gain_mlp, shift_mlp=shift_mlp)


EPSILON = 1e-05
MASKED = -1e+30
HIGHEST = lax.Precision.HIGHEST

@jax.custom_vjp
def low(v):
    return lax.optimization_barrier(v.astype(jnp.bfloat16)).astype(jnp.float32)

@jax.custom_vjp
def low_back(v):
    return v

def low_keep(v):
    return (low(v), None)

def low_pass(kept, grad):
    return (grad,)

def back_keep(v):
    return (v, None)

def back_low(kept, grad):
    return (low(grad),)
low.defvjp(low_keep, low_pass)
low_back.defvjp(back_keep, back_low)

def layer_norm(values, gain_vector, shift_vector):
    row_mean = lax.optimization_barrier(jnp.mean(values, axis=-1, keepdims=True))
    centred = values - row_mean
    spread = lax.optimization_barrier(jnp.mean(centred * centred, axis=-1, keepdims=True))
    return centred * lax.rsqrt(spread + EPSILON) * gain_vector + shift_vector

def positions(block_order, first_row, row_count, half_rows):
    row_index = first_row + lax.iota(jnp.int32, row_count)
    slot_index = row_index // half_rows
    slot_table = lax.iota(jnp.int32, block_order.shape[0])
    picked = lax.optimization_barrier(jnp.sum(jnp.where(slot_index[:, None] == slot_table[None, :], block_order[None, :], 0), axis=1))
    return (picked * half_rows + row_index % half_rows).astype(jnp.int32)

def rotary_tables(places):
    half_rot = ROT // 2
    frequency = jnp.exp(-math.log(10000.0) * (2.0 * jnp.arange(half_rot, dtype=jnp.float32)) / ROT)
    angles = places.astype(jnp.float32)[:, None] * frequency[None, :]
    angles = jnp.concatenate([angles, angles], axis=1)
    return (jnp.cos(angles), jnp.sin(angles))

def rotate(heads_part, cosine_table, sine_table):
    half_rot = ROT // 2
    turned_part = heads_part[..., :ROT]
    turned = jnp.concatenate([-turned_part[..., half_rot:], turned_part[..., :half_rot]], axis=-1)
    spun_part = turned_part * cosine_table[:, None, :] + turned * sine_table[:, None, :]
    return jnp.concatenate([spun_part, heads_part[..., ROT:]], axis=-1)

def attend_block(query_block, query_places, keys, values, key_places):
    scale_factor = 1.0 / math.sqrt(HEAD)
    scores = jnp.einsum('qhd,khd->hqk', query_block, keys, precision=HIGHEST) * scale_factor
    scores = low_back(scores)
    visible = key_places[None, None, :] <= query_places[None, :, None]
    scores = jnp.where(visible, scores, MASKED)
    top_score = lax.optimization_barrier(jnp.max(scores, axis=-1, keepdims=True))
    expd = jnp.exp(scores - top_score)
    weights = low(expd / lax.optimization_barrier(jnp.sum(expd, axis=-1, keepdims=True)))
    return jnp.einsum('hqk,khd->qhd', weights, values, precision=HIGHEST)

def forward(tokens, w_qkv, b_qkv, w_dense, b_dense, w_up, b_up, w_down, b_down, gain_attn, shift_attn, gain_mlp, shift_mlp, places):
    seq_rows = tokens.shape[0]
    ln_attn = low(layer_norm(tokens, gain_attn, shift_attn))
    ln_mlp = low(layer_norm(tokens, gain_mlp, shift_mlp))
    joined_proj = low_back(jnp.dot(ln_attn, w_qkv, precision=HIGHEST) + b_qkv)
    joined_proj = joined_proj.reshape(seq_rows, HEADS, 3, HEAD)
    cosine_table, sine_table = rotary_tables(places)
    queries = low(rotate(joined_proj[:, :, 0], cosine_table, sine_table))
    keys = low(rotate(joined_proj[:, :, 1], cosine_table, sine_table))
    values = low(joined_proj[:, :, 2])
    block_rows = 512 if seq_rows % 512 == 0 else seq_rows
    block_count = seq_rows // block_rows
    query_blocks = queries.reshape(block_count, block_rows, HEADS, HEAD)
    place_blocks = places.reshape(block_count, block_rows)

    def block_step(block_pair):
        return attend_block(block_pair[0], block_pair[1], keys, values, places)
    attended = lax.map(jax.checkpoint(block_step), (query_blocks, place_blocks))
    attended = attended.reshape(seq_rows, HEADS * HEAD)
    attended = low_back(low(attended))
    upward = low_back(jnp.dot(ln_mlp, w_up, precision=HIGHEST) + b_up)
    hidden = low(jax.nn.gelu(upward, approximate=False))
    attn_out = jnp.dot(attended, w_dense, precision=HIGHEST) + b_dense
    mlp_out = jnp.dot(hidden, w_down, precision=HIGHEST) + b_down
    return tokens + attn_out + mlp_out

def reference(tokens, block_order, cotangent, w_qkv, b_qkv, w_dense, b_dense, w_up, b_up, w_down, b_down, gain_attn, shift_attn, gain_mlp, shift_mlp):
    places = positions(block_order, 0, tokens.shape[0], HALF)

    def apply_layer(*parameters):
        return forward(*parameters, places)
    output, pullback = jax.vjp(apply_layer, tokens.astype(jnp.float32), w_qkv.astype(jnp.float32), b_qkv, w_dense.astype(jnp.float32), b_dense, w_up.astype(jnp.float32), b_up, w_down.astype(jnp.float32), b_down, gain_attn, shift_attn, gain_mlp, shift_mlp)
    gradients = pullback(cotangent.astype(jnp.float32))
    return (output.astype(jnp.bfloat16), gradients[0].astype(jnp.bfloat16), gradients[1], gradients[2], gradients[3], gradients[4], gradients[5], gradients[6], gradients[7], gradients[8], gradients[9], gradients[10], gradients[11], gradients[12])
```

```python
import functools
import math

import jax
import jax.numpy as jnp
import numpy as np
from jax import lax
from jax.experimental import pallas as pl
from jax.experimental.pallas import tpu as pltpu
from jax.sharding import Mesh
from jax.sharding import PartitionSpec as P

HEAD = 64
ROT = 16
HEADS = 3
EPSILON = 1e-05
MASKED = -1e30
CTX = ("xl", "z", "y")
TP = ("xh", "c")
F32 = jnp.float32
BF = jnp.bfloat16
LOG2E = math.log2(math.e)
SCALE = 1.0 / math.sqrt(HEAD)
SCORE = SCALE * LOG2E
NT = (((1,), (1,)), ((), ()))
TN = (((0,), (0,)), ((), ()))


def mm(a, b):
    return jnp.dot(a, b, preferred_element_type=F32)


def mm_nt(a, b):
    return lax.dot_general(a, b, NT, preferred_element_type=F32)


def mm_tn(a, b):
    return lax.dot_general(a, b, TN, preferred_element_type=F32)


def lane_table():
    lane = np.arange(128) % HEAD
    table = np.zeros((8, 128), np.float32)
    table[0] = np.where(lane < ROT, 10000.0 ** (-2.0 * (lane % 8) / ROT), 0.0)
    table[1] = lane < 8
    table[2] = (lane >= 8) & (lane < ROT)
    return table


def spin_tables(coords, order, table):
    shard = (coords[0] * 4 + coords[1]) * 4 + coords[2]
    step = lax.broadcasted_iota(jnp.int32, (128, 128), 0)
    places = jnp.concatenate(
        [step + order[2 * shard] * 128, step + order[2 * shard + 1] * 128], axis=0
    )
    angles = places.astype(F32) * table[0:1, :]
    sine = jnp.sin(angles)
    return jnp.cos(angles), sine * -table[1:2, :], sine * table[2:3, :]


def normed(tokens):
    values = tokens.astype(F32)
    centred = values - jnp.mean(values, axis=-1, keepdims=True)
    rstd = lax.rsqrt(jnp.mean(centred * centred, axis=-1, keepdims=True) + EPSILON)
    return centred * rstd, rstd


def front_kernel(
    coords, order, table, tok, cot, wqkv, bqkv, wd, ga, sa, gm, sm, qdo, kv, lna, lnm
):
    xhat, _ = normed(tok[...])
    ln = (xhat * ga[...] + sa[...]).astype(BF)
    lna[...] = ln
    lnm[...] = (xhat * gm[...] + sm[...]).astype(BF)
    joined = mm(ln, wqkv[...]) + bqkv[...]
    cosine, left_sine, right_sine = spin_tables(coords, order, table)
    half = lax.broadcasted_iota(jnp.int32, (256, 128), 1) < HEAD
    tiles = []
    for t in range(4):
        x = joined[:, 128 * t : 128 * t + 128]
        spun = (
            x * cosine + pltpu.roll(x, 120, 1) * left_sine + pltpu.roll(x, 8, 1) * right_sine
        )
        if t == 1:
            spun = jnp.where(half, x, spun)
        if t == 2:
            spun = jnp.where(half, spun, x)
        tiles.append(spun)
    pieces = []
    for t in range(4):
        pieces += [tiles[t][:, :HEAD], tiles[t][:, HEAD:]]
    pieces.append(joined[:, 512:576])
    d_att = mm_nt(cot[...], wd[...])
    qdo[...] = jnp.concatenate(
        [pieces[0], pieces[3], pieces[6], d_att], axis=1
    ).astype(BF)
    kv[...] = jnp.concatenate([pieces[i] for i in (1, 4, 7, 2, 5, 8)], axis=1).astype(BF)


def mlp_kernel(ln, cot, wu, bu, wdn, gw, small, part, d_ln):
    up = mm(ln[...], wu[...]) + bu[...]
    phi = 0.5 * (1.0 + lax.erf(up * math.sqrt(0.5)))
    hid = (up * phi).astype(BF)
    slope = phi + up * (jnp.exp(up * up * -0.5) * (1.0 / math.sqrt(2.0 * math.pi)))
    d_up = (mm_nt(cot[...], wdn[...]) * slope).astype(BF)
    gw[0:768, :] = mm_tn(ln[...], d_up).astype(BF)
    gw[768:1536, :] = mm_tn(hid, cot[...]).astype(BF)
    part[...] = mm(hid, wdn[...])
    d_ln[...] = mm_nt(d_up, wu[...])
    small[0:1, :] = jnp.sum(d_up.astype(F32), axis=0, keepdims=True)
    small[1:2, :] = jnp.sum(cot[...].astype(F32), axis=0, keepdims=True)
    small[2:8, :] = jnp.zeros((6, 768), F32)


def mask_tile(scores, gap, q_places, k_places):
    rows = []
    for kb in range(2):
        cells = []
        for qb in range(2):
            cell = scores[128 * kb : 128 * kb + 128, 128 * qb : 128 * qb + 128]
            cells.append(jnp.where(gap <= (q_places[qb] - k_places[kb]) * 128, cell, MASKED))
        rows.append(jnp.concatenate(cells, axis=1))
    return jnp.concatenate(rows, axis=0)


def gap_table():
    return lax.broadcasted_iota(jnp.int32, (128, 128), 0) - lax.broadcasted_iota(
        jnp.int32, (128, 128), 1
    )


def query_places(coords, order, slot):
    shard = (coords[0] * 4 + coords[1]) * 4 + (coords[2] + slot) % 4
    return order[2 * shard], order[2 * shard + 1]


def key_places(coords, order, tile):
    shard = ((coords[0] + tile % 2) % 2 * 4 + (coords[1] + tile // 2) % 4) * 4 + coords[2]
    return order[2 * shard], order[2 * shard + 1]


def forward_kernel(
    coords, order, q0, q1, q2, q3, k0, k1, k2, k3, o0, o1, o2, o3, stats, qs, os
):
    for j, ref in enumerate((q0, q1, q2, q3)):
        qs[j] = ref[...]
    keys = (k0, k1, k2, k3)
    gap = gap_table()

    def slot_step(j, carry):
        q_places = query_places(coords, order, j)
        for h in range(HEADS):
            query = qs[j, :, HEAD * h : HEAD * h + HEAD]
            d_att = qs[j, :, 192 + HEAD * h : 256 + HEAD * h]
            tiles, tops = [], []
            for t in range(8):
                key = keys[t // 2][t % 2, :, HEAD * h : HEAD * h + HEAD]
                scores = mask_tile(
                    mm_nt(key, query), gap, q_places, key_places(coords, order, t)
                )
                tiles.append(scores)
                tops.append(jnp.max(scores, axis=0, keepdims=True))
            top = functools.reduce(jnp.maximum, tops) * SCORE
            total = jnp.zeros((1, 256), F32)
            out = jnp.zeros((HEAD, 256), F32)
            for t in range(8):
                weights = jnp.exp2(tiles[t] * SCORE - top)
                total = total + jnp.sum(weights, axis=0, keepdims=True)
                value = keys[t // 2][t % 2, :, 192 + HEAD * h : 256 + HEAD * h]
                out = out + mm(value.T, weights.astype(BF))
            out = out / total
            os[j, HEAD * h : HEAD * h + HEAD, :] = out.astype(BF)
            stats[j, h : h + 1, :] = top + jnp.log2(total)
            stats[j, 3 + h : 4 + h, :] = jnp.sum(
                d_att.astype(F32).T * out, axis=0, keepdims=True
            )
        stats[j, 6:8, :] = jnp.zeros((2, 256), F32)
        return carry

    lax.fori_loop(0, 4, slot_step, 0)
    for j, ref in enumerate((o0, o1, o2, o3)):
        ref[...] = os[j]


def merge_kernel(s0, s1, s2, s3, o0, o1, o2, o3, wd, part, att, branch):
    stats = [ref[-step % 4] for step, ref in enumerate((s0, s1, s2, s3))]
    outs = [o0, o3, o2, o1]
    rows = []
    for h in range(HEADS):
        logs = [s[h : h + 1, :] for s in stats]
        top = functools.reduce(jnp.maximum, logs)
        shares = [jnp.exp2(v - top) for v in logs]
        total = functools.reduce(jnp.add, shares)
        mixed = functools.reduce(
            jnp.add,
            [
                share * ref[HEAD * h : HEAD * h + HEAD, :].astype(F32)
                for share, ref in zip(shares, outs, strict=True)
            ],
        )
        rows.append(mixed / total)
    att_low = jnp.concatenate(rows, axis=0).T.astype(BF)
    att[...] = att_low
    branch[...] = (mm(att_low, wd[...]) + part[...]).astype(BF)


def backward_kernel(
    coords, order, s0, s1, s2, s3, q0, q1, q2, q3, k0, k1, k2, k3,
    dq0, dq1, dq2, dq3, dk0, dk1, dk2, dk3, ks, dks, dqs, st,
):
    queries = (q0, q1, q2, q3)
    for b, ref in enumerate((k0, k1, k2, k3)):
        ks[2 * b : 2 * b + 2] = ref[...]
    dqs[...] = jnp.zeros_like(dqs)
    for j in range(4):
        parts = [ref[(j - step) % 4] for step, ref in enumerate((s0, s1, s2, s3))]
        logs = [p[0:3, :] for p in parts]
        top = functools.reduce(jnp.maximum, logs)
        total = functools.reduce(jnp.add, [jnp.exp2(v - top) for v in logs])
        whole = top + jnp.log2(total)
        st[j, 0:3, :] = whole
        st[j, 3:6, :] = functools.reduce(
            jnp.add, [jnp.exp2(p[0:3, :] - whole) * p[3:6, :] for p in parts]
        )
    gap = gap_table()

    def tile_step(t, carry):
        k_places = key_places(coords, order, t)
        for h in range(HEADS):
            key = ks[t, :, HEAD * h : HEAD * h + HEAD]
            value = ks[t, :, 192 + HEAD * h : 256 + HEAD * h]
            key_turned = key.T
            d_key = jnp.zeros((256, HEAD), F32)
            d_value = jnp.zeros((256, HEAD), F32)
            for j in range(4):
                query = queries[j][:, HEAD * h : HEAD * h + HEAD]
                d_att = queries[j][:, 192 + HEAD * h : 256 + HEAD * h]
                scores = mask_tile(
                    mm_nt(key, query), gap, query_places(coords, order, j), k_places
                )
                weights = jnp.exp2(scores * SCORE - st[j, h : h + 1, :])
                d_weights = mm_nt(value, d_att)
                d_scores = (weights * (d_weights - st[j, 3 + h : 4 + h, :])).astype(BF)
                d_value = d_value + mm(weights.astype(BF), d_att)
                d_key = d_key + mm(d_scores, query)
                dqs[j, HEAD * h : HEAD * h + HEAD, :] += mm(key_turned, d_scores)
            dks[t, :, HEAD * h : HEAD * h + HEAD] = (d_key * SCALE).astype(BF)
            dks[t, :, 192 + HEAD * h : 256 + HEAD * h] = d_value.astype(BF)
        return carry

    lax.fori_loop(0, 8, tile_step, 0)
    for j, ref in enumerate((dq0, dq1, dq2, dq3)):
        ref[...] = (dqs[j] * SCALE).astype(BF)
    for b, ref in enumerate((dk0, dk1, dk2, dk3)):
        ref[...] = dks[2 * b : 2 * b + 2]


def tail_kernel(
    coords, order, table, tok, cot, lna, wqkv, ga, gm, dq0, dq1, dq2, dq3, dkv0, dkv1,
    att, d_ln_mlp, small_in, g0, g1, g2, g3, upstream, small,
):
    d_query = (
        dq0[...].astype(F32) + dq1[...].astype(F32) + dq2[...].astype(F32) + dq3[...].astype(F32)
    ).T
    d_kv = dkv0[...].astype(F32) + dkv1[...].astype(F32)
    both = jnp.concatenate([d_query, d_kv[:, :192]], axis=1)
    cosine, left_sine, right_sine = spin_tables(coords, order, table)
    pieces = []
    for t in range(3):
        x = both[:, 128 * t : 128 * t + 128]
        back = (
            x * cosine
            + pltpu.roll(x * left_sine, 8, 1)
            + pltpu.roll(x * right_sine, 120, 1)
        )
        pieces += [back[:, :HEAD], back[:, HEAD:]]
    cols = []
    for h in range(HEADS):
        cols += [pieces[h], pieces[3 + h], d_kv[:, 192 + HEAD * h : 256 + HEAD * h]]
    d_joined = jnp.concatenate(cols, axis=1).astype(BF)
    grads = jnp.concatenate(
        [mm_tn(lna[...], d_joined), mm_tn(cot[...], att[...])], axis=1
    ).astype(BF)
    y = coords[2]
    for slot, ref in enumerate((g0, g1, g2, g3)):
        pass
    for piece in range(4):
        for slot, ref in enumerate((g0, g1, g2, g3)):

            @pl.when((y + slot) % 4 == piece)
            def _(ref=ref, piece=piece):
                ref[...] = grads[192 * piece : 192 * piece + 192, :]

    d_attn = mm_nt(d_joined, wqkv[...])
    d_mlp = d_ln_mlp[...]
    xhat, _ = normed(tok[...])
    upstream[...] = (d_attn * ga[...] + d_mlp * gm[...]).astype(BF)
    small[0:2, :] = small_in[0:2, :]
    small[2:3, :] = jnp.sum(d_attn * xhat, axis=0, keepdims=True)
    small[3:4, :] = jnp.sum(d_attn, axis=0, keepdims=True)
    small[4:5, :] = jnp.sum(d_mlp * xhat, axis=0, keepdims=True)
    small[5:6, :] = jnp.sum(d_mlp, axis=0, keepdims=True)
    small[6:7, 0:576] = jnp.sum(d_joined.astype(F32), axis=0, keepdims=True)
    small[6:7, 576:768] = jnp.zeros((1, 192), F32)
    small[7:8, :] = jnp.zeros((1, 768), F32)


def token_kernel(tok, cot, e0, e1, out):
    xhat, rstd = normed(tok[...])
    e = e0[...].astype(F32) + e1[...].astype(F32)
    inner = e - jnp.mean(e, axis=-1, keepdims=True)
    inner = inner - xhat * jnp.mean(e * xhat, axis=-1, keepdims=True)
    out[...] = (cot[...].astype(F32) + rstd * inner).astype(BF)


def assemble_kernel(coords, p0, p1, p2, p3, gq, gd, whole):
    for slot, ref in enumerate((p0, p1, p2, p3)):
        whole[(coords[2] + slot) % 4] = ref[...].astype(F32)
    for piece in range(4):
        gq[192 * piece : 192 * piece + 192, :] = whole[piece, :, 0:576]
        gd[:, 192 * piece : 192 * piece + 192] = whole[piece, :, 576:768].T


def call(kernel, outs, args, scalars, scratch=(), flops=0, mib=48):
    smem = pl.BlockSpec(memory_space=pltpu.SMEM)
    vmem = pl.BlockSpec(memory_space=pltpu.VMEM)
    shapes = [jax.ShapeDtypeStruct(s, d) for s, d in outs]
    moved = sum(math.prod(s) * np.dtype(d).itemsize for s, d in outs) + sum(
        a.size * a.dtype.itemsize for a in args
    )
    return pl.pallas_call(
        kernel,
        out_shape=shapes,
        in_specs=[smem] * scalars + [vmem] * (len(args) - scalars),
        out_specs=[vmem] * len(shapes),
        scratch_shapes=list(scratch),
        compiler_params=pltpu.CompilerParams(vmem_limit_bytes=mib << 20),
        cost_estimate=pl.CostEstimate(flops=flops, bytes_accessed=moved, transcendentals=0),
    )(*args)


def hop(x, axis, step):
    n = lax.axis_size(axis)
    return lax.ppermute(x, axis, [(i, (i + step) % n) for i in range(n)])


def add(*parts):
    return functools.reduce(jnp.add, [p.astype(F32) for p in parts])


def on_device(
    tokens,
    block_order,
    cotangent,
    w_qkv,
    b_qkv,
    w_dense,
    b_dense,
    w_up,
    b_up,
    w_down,
    b_down,
    gain_attn,
    shift_attn,
    gain_mlp,
    shift_mlp,
):
    coords = jnp.stack([lax.axis_index(a) for a in CTX]).astype(jnp.int32)
    table = jnp.asarray(lane_table())

    def row(v):
        return v.reshape(1, -1)

    qdo, kv, ln_attn, ln_mlp = call(
        front_kernel,
        [((256, 384), BF), ((256, 384), BF), ((256, 768), BF), ((256, 768), BF)],
        (coords, block_order, table, tokens, cotangent, w_qkv, row(b_qkv), w_dense,
         row(gain_attn), row(shift_attn), row(gain_mlp), row(shift_mlp)),
        2,
        flops=8 * 10**8,
    )
    kv0 = jnp.stack([kv, hop(kv, "xl", 1)])
    kvs = [kv0] + [hop(kv0, "z", -b) for b in (1, 3, 2)]
    kvs = [kvs[0], kvs[1], kvs[3], kvs[2]]
    qdos = [qdo] + [hop(qdo, "y", -j) for j in (1, 2, 3)]

    grads_mlp, small_mlp, part_mlp, d_ln_mlp = call(
        mlp_kernel,
        [((1536, 768), BF), ((8, 768), F32), ((256, 768), F32), ((256, 768), F32)],
        (ln_mlp, cotangent, w_up, row(b_up), w_down),
        0,
        flops=24 * 10**8,
    )
    grads_mlp = lax.psum_scatter(grads_mlp, ("z", "y"), scatter_dimension=0, tiled=True)
    grads_mlp = lax.psum(grads_mlp, "xl")
    grads_mlp = lax.all_gather(grads_mlp, ("z", "y"), axis=0, tiled=True)

    *outs, stats = call(
        forward_kernel,
        [((192, 256), BF)] * 4 + [((4, 8, 256), F32)],
        (coords, block_order, *qdos, *kvs),
        2,
        scratch=[pltpu.VMEM((4, 256, 384), BF), pltpu.VMEM((4, 192, 256), BF)],
        flops=64 * 10**8,
    )
    stats_all = [stats] + [hop(stats, "y", -j) for j in (1, 2, 3)]
    outs = [outs[0]] + [hop(outs[j], "y", j) for j in (1, 2, 3)]
    att, branch = call(
        merge_kernel,
        [((256, 192), BF), ((256, 768), BF)],
        (*stats_all, *outs, w_dense, part_mlp),
        0,
        flops=10**8,
    )
    branch = add(branch, hop(branch, "c", 1)).astype(BF)
    branch = add(branch, hop(branch, "xh", 1))
    output = (tokens.astype(F32) + branch + b_dense + b_down).astype(BF)

    grads = call(
        backward_kernel,
        [((192, 256), BF)] * 4 + [((2, 256, 384), BF)] * 4,
        (coords, block_order, *stats_all, *qdos, *kvs),
        2,
        scratch=[
            pltpu.VMEM((8, 256, 384), BF),
            pltpu.VMEM((8, 256, 384), BF),
            pltpu.VMEM((4, 192, 256), F32),
            pltpu.VMEM((4, 8, 256), F32),
        ],
        flops=160 * 10**8,
    )
    d_kvs = [grads[4]] + [hop(grads[4 + b], "z", b) for b in (1, 3, 2)]
    d_queries = [grads[0]] + [hop(grads[j], "y", j) for j in (1, 2, 3)]
    d_kv_own = add(*[d[0] for d in d_kvs]).astype(BF)
    d_kv_other = hop(add(*[d[1] for d in d_kvs]).astype(BF), "xl", 1)
    *pieces, upstream, small = call(
        tail_kernel,
        [((192, 768), BF)] * 4 + [((256, 768), BF), ((8, 768), F32)],
        (coords, block_order, table, tokens, cotangent, ln_attn, w_qkv, row(gain_attn),
         row(gain_mlp), *d_queries, d_kv_own, d_kv_other, att, d_ln_mlp, small_mlp),
        2,
        flops=8 * 10**8,
    )

    piece = add(pieces[0], *[hop(pieces[j], "y", j) for j in (1, 2, 3)])
    piece = piece.astype(BF).reshape(4, 48, 768)
    z = lax.axis_index("z")

    def block(j):
        return lax.dynamic_index_in_dim(piece, (z + j) % 4, 0, keepdims=False)

    third = add(block(0), *[hop(block(j), "z", j) for j in (1, 2, 3)]).astype(BF)
    third = add(third, hop(third, "xl", 1)).astype(BF)
    quarter = jnp.zeros((4, 48, 768), BF)
    for j, part in enumerate([third] + [hop(third, "z", -j) for j in (1, 2, 3)]):
        quarter = lax.dynamic_update_index_in_dim(quarter, part, (z + j) % 4, 0)
    quarter = quarter.reshape(192, 768)
    grad_w_qkv, grad_w_dense = call(
        assemble_kernel,
        [((768, 576), F32), ((192, 768), F32)],
        (coords, quarter, *[hop(quarter, "y", -j) for j in (1, 2, 3)]),
        1,
        scratch=[pltpu.VMEM((4, 192, 768), F32)],
    )

    upstream = add(upstream, hop(upstream, "c", 1)).astype(BF)
    (grad_tokens,) = call(
        token_kernel,
        [((256, 768), BF)],
        (tokens, cotangent, upstream, hop(upstream, "xh", 1)),
        0,
    )

    gains = small[2:6]
    gains = gains + hop(gains, "c", 1)
    gains = gains + hop(gains, "xh", 1)
    small = jnp.concatenate([small[0:2], gains, small[6:8]], axis=0)
    small = small + hop(small, "xl", 1)
    for axis in ("y", "z"):
        small = add(small, *[hop(small, axis, j) for j in (1, 2, 3)])

    return (
        output,
        grad_tokens,
        grad_w_qkv,
        small[6, :576],
        grad_w_dense,
        small[1],
        grads_mlp[:768].astype(F32),
        small[0],
        grads_mlp[768:].astype(F32),
        small[1],
        small[2],
        small[3],
        small[4],
        small[5],
    )


def solution(mesh):
    fine = Mesh(mesh.devices.reshape(2, 4, 4, 2, 2), CTX + TP)
    rows, cols = P(CTX, None), P(None, TP)
    return jax.shard_map(
        on_device,
        mesh=fine,
        in_specs=(
            rows, P(), rows, cols, P(TP), P(TP, None), P(), cols, P(TP), P(TP, None),
            P(), P(), P(), P(), P(),
        ),
        out_specs=(
            rows, rows, cols, P(TP), P(TP, None), P(), cols, P(TP), P(TP, None),
            P(), P(), P(), P(), P(),
        ),
        check_vma=False,
    )
```

```python
import functools
import math

import jax
import jax.numpy as jnp
import numpy as np
from jax import lax
from jax.experimental import pallas as pl
from jax.experimental.pallas import tpu as pltpu
from jax.sharding import Mesh
from jax.sharding import PartitionSpec as P

HEAD = 64
ROT = 16
HEADS = 3
EPSILON = 1e-05
MASKED = -1e30
CTX = ("xl", "z", "y")
TP = ("xh", "c")
F32 = jnp.float32
BF = jnp.bfloat16
LOG2E = math.log2(math.e)
SCALE = 1.0 / math.sqrt(HEAD)
SCORE = SCALE * LOG2E
NT = (((1,), (1,)), ((), ()))
TN = (((0,), (0,)), ((), ()))


def mm(a, b):
    return jnp.dot(a, b, preferred_element_type=F32)


def mm_nt(a, b):
    return lax.dot_general(a, b, NT, preferred_element_type=F32)


def mm_tn(a, b):
    return lax.dot_general(a, b, TN, preferred_element_type=F32)


def lane_table():
    lane = np.arange(128) % HEAD
    table = np.zeros((8, 128), np.float32)
    table[0] = np.where(lane < ROT, 10000.0 ** (-2.0 * (lane % 8) / ROT), 0.0)
    table[1] = lane < 8
    table[2] = (lane >= 8) & (lane < ROT)
    return table


def spin_tables(coords, order, table):
    shard = (coords[0] * 4 + coords[1]) * 4 + coords[2]
    step = lax.broadcasted_iota(jnp.int32, (128, 128), 0)
    places = jnp.concatenate(
        [step + order[2 * shard] * 128, step + order[2 * shard + 1] * 128], axis=0
    )
    angles = places.astype(F32) * table[0:1, :]
    sine = jnp.sin(angles)
    return jnp.cos(angles), sine * -table[1:2, :], sine * table[2:3, :]


def row(ref):
    return ref[...].reshape(1, -1)


def keep_kernel(x, after, out):
    out[...] = x[...]


def widen_kernel(x, after, up, down):
    up[...] = x[0:768, :].astype(F32)
    down[...] = x[768:1536, :].astype(F32)


def normed(tokens):
    values = tokens.astype(F32)
    centred = values - jnp.mean(values, axis=-1, keepdims=True)
    rstd = lax.rsqrt(jnp.mean(centred * centred, axis=-1, keepdims=True) + EPSILON)
    return centred * rstd, rstd


def front_kernel(
    coords, order, table, tok, cot, wqkv, wd, ga, sa, gm, sm, bqkv, qdo, kv, lna, lnm
):
    xhat, _ = normed(tok[...])
    ln = (xhat * row(ga) + row(sa)).astype(BF)
    lna[...] = ln
    lnm[...] = (xhat * row(gm) + row(sm)).astype(BF)
    joined = mm_nt(ln, wqkv[...]) + row(bqkv)
    cosine, left_sine, right_sine = spin_tables(coords, order, table)
    half = lax.broadcasted_iota(jnp.int32, (256, 128), 1) < HEAD
    tiles = []
    for t in range(4):
        x = joined[:, 128 * t : 128 * t + 128]
        spun = (
            x * cosine + pltpu.roll(x, 120, 1) * left_sine + pltpu.roll(x, 8, 1) * right_sine
        )
        if t == 1:
            spun = jnp.where(half, x, spun)
        if t == 2:
            spun = jnp.where(half, spun, x)
        tiles.append(spun)
    pieces = []
    for t in range(4):
        pieces += [tiles[t][:, :HEAD], tiles[t][:, HEAD:]]
    pieces.append(joined[:, 512:576])
    d_att = mm_nt(cot[...], wd[...])
    qdo[...] = jnp.concatenate(
        [pieces[0], pieces[3], pieces[6], d_att], axis=1
    ).astype(BF)
    kv[...] = jnp.concatenate([pieces[i] for i in (1, 4, 7, 2, 5, 8)], axis=1).astype(BF)


def mlp_kernel(ln, cot, wu, bu, wdn, after, gw, small, part, d_ln):
    up = mm(ln[...], wu[...]) + row(bu)
    phi = 0.5 * (1.0 + lax.erf(up * math.sqrt(0.5)))
    hid = (up * phi).astype(BF)
    slope = phi + up * (jnp.exp(up * up * -0.5) * (1.0 / math.sqrt(2.0 * math.pi)))
    d_up = (mm_nt(cot[...], wdn[...]) * slope).astype(BF)
    gw[0:768, :] = mm_tn(ln[...], d_up).astype(BF)
    gw[768:1536, :] = mm_tn(hid, cot[...]).astype(BF)
    part[...] = mm(hid, wdn[...])
    d_ln[...] = mm_nt(d_up, wu[...])
    small[0:1, :] = jnp.sum(d_up.astype(F32), axis=0, keepdims=True)
    small[1:2, :] = jnp.sum(cot[...].astype(F32), axis=0, keepdims=True)
    small[2:8, :] = jnp.zeros((6, 768), F32)


def mask_tile(scores, gap, q_places, k_places):
    rows = []
    for kb in range(2):
        cells = []
        for qb in range(2):
            cell = scores[128 * kb : 128 * kb + 128, 128 * qb : 128 * qb + 128]
            cells.append(jnp.where(gap <= (q_places[qb] - k_places[kb]) * 128, cell, MASKED))
        rows.append(jnp.concatenate(cells, axis=1))
    return jnp.concatenate(rows, axis=0)


def gap_table():
    return lax.broadcasted_iota(jnp.int32, (128, 128), 0) - lax.broadcasted_iota(
        jnp.int32, (128, 128), 1
    )


def query_places(coords, order, slot):
    shard = (coords[0] * 4 + coords[1]) * 4 + (coords[2] + slot) % 4
    return order[2 * shard], order[2 * shard + 1]


def key_places(coords, order, tile):
    shard = ((coords[0] + tile % 2) % 2 * 4 + (coords[1] + tile // 2) % 4) * 4 + coords[2]
    return order[2 * shard], order[2 * shard + 1]


def forward_kernel(coords, order, *refs):
    queries, keys = refs[0:4], refs[4:12]
    outs, stats, qs, os = refs[12:16], refs[16], refs[17], refs[18]
    for j, ref in enumerate(queries):
        qs[j] = ref[...]
    gap = gap_table()

    def slot_step(j, carry):
        q_places = query_places(coords, order, j)
        for h in range(HEADS):
            query = qs[j, :, HEAD * h : HEAD * h + HEAD]
            d_att = qs[j, :, 192 + HEAD * h : 256 + HEAD * h]
            tiles, tops = [], []
            for t in range(8):
                key = keys[t][:, HEAD * h : HEAD * h + HEAD]
                scores = mask_tile(
                    mm_nt(key, query), gap, q_places, key_places(coords, order, t)
                )
                tiles.append(scores)
                tops.append(jnp.max(scores, axis=0, keepdims=True))
            top = functools.reduce(jnp.maximum, tops) * SCORE
            total = jnp.zeros((1, 256), F32)
            out = jnp.zeros((HEAD, 256), F32)
            for t in range(8):
                weights = jnp.exp2(tiles[t] * SCORE - top)
                total = total + jnp.sum(weights, axis=0, keepdims=True)
                value = keys[t][:, 192 + HEAD * h : 256 + HEAD * h]
                out = out + mm(value.T, weights.astype(BF))
            out = out / total
            os[j, HEAD * h : HEAD * h + HEAD, :] = out.astype(BF)
            stats[j, h : h + 1, :] = top + jnp.log2(total)
            stats[j, 3 + h : 4 + h, :] = jnp.sum(
                d_att.astype(F32).T * out, axis=0, keepdims=True
            )
        stats[j, 6:8, :] = jnp.zeros((2, 256), F32)
        return carry

    lax.fori_loop(0, 4, slot_step, 0)
    for j, ref in enumerate(outs):
        ref[...] = os[j]


def merge_kernel(s0, s1, s2, s3, o0, o1, o2, o3, wd, part, att, branch):
    stats = [ref[-step % 4] for step, ref in enumerate((s0, s1, s2, s3))]
    outs = [o0, o3, o2, o1]
    rows = []
    for h in range(HEADS):
        logs = [s[h : h + 1, :] for s in stats]
        top = functools.reduce(jnp.maximum, logs)
        shares = [jnp.exp2(v - top) for v in logs]
        total = functools.reduce(jnp.add, shares)
        mixed = functools.reduce(
            jnp.add,
            [
                share * ref[HEAD * h : HEAD * h + HEAD, :].astype(F32)
                for share, ref in zip(shares, outs, strict=True)
            ],
        )
        rows.append(mixed / total)
    att_low = jnp.concatenate(rows, axis=0).T.astype(BF)
    att[...] = att_low
    branch[...] = (mm(att_low, wd[...]) + part[...]).astype(BF)


def backward_kernel(tiles, first, last, unread, coords, order, *refs):
    n = len(tiles)
    refs = list(refs)

    def take(count):
        taken = refs[:count]
        del refs[:count]
        return taken

    stats = take(4 if first else 1)
    queries, keys = take(4), take(n)
    d_before = None if first else take(1)[0]
    take(unread)
    if first:
        (st,) = take(1)
    else:
        (st,) = stats
    d_keys = take(n // 2)
    d_queries = take(4 if last else 1)
    ks, dks = take(2)
    dqs = take(1)[0] if last else d_queries[0]
    for i, ref in enumerate(keys):
        ks[i] = ref[...]
    dqs[...] = jnp.zeros_like(dqs) if first else d_before[...]
    for j in range(4 if first else 0):
        parts = [ref[(j - step) % 4] for step, ref in enumerate(stats)]
        logs = [p[0:3, :] for p in parts]
        top = functools.reduce(jnp.maximum, logs)
        total = functools.reduce(jnp.add, [jnp.exp2(v - top) for v in logs])
        whole = top + jnp.log2(total)
        st[j, 0:3, :] = whole
        st[j, 3:6, :] = functools.reduce(
            jnp.add, [jnp.exp2(p[0:3, :] - whole) * p[3:6, :] for p in parts]
        )
        st[j, 6:8, :] = jnp.zeros((2, 256), F32)
    gap = gap_table()

    def tile_step(i, carry):
        step = tiles[2] - tiles[0] if n > 2 else 0
        k_places = key_places(coords, order, tiles[0] + i % 2 + i // 2 * step)
        for h in range(HEADS):
            key = ks[i, :, HEAD * h : HEAD * h + HEAD]
            value = ks[i, :, 192 + HEAD * h : 256 + HEAD * h]
            key_turned = key.T
            d_key = jnp.zeros((256, HEAD), F32)
            d_value = jnp.zeros((256, HEAD), F32)
            for j in range(4):
                query = queries[j][:, HEAD * h : HEAD * h + HEAD]
                d_att = queries[j][:, 192 + HEAD * h : 256 + HEAD * h]
                scores = mask_tile(
                    mm_nt(key, query), gap, query_places(coords, order, j), k_places
                )
                weights = jnp.exp2(scores * SCORE - st[j, h : h + 1, :])
                d_weights = mm_nt(value, d_att)
                d_scores = (weights * (d_weights - st[j, 3 + h : 4 + h, :])).astype(BF)
                d_value = d_value + mm(weights.astype(BF), d_att)
                d_key = d_key + mm(d_scores, query)
                dqs[j, HEAD * h : HEAD * h + HEAD, :] += mm(key_turned, d_scores)
            dks[i, :, HEAD * h : HEAD * h + HEAD] = (d_key * SCALE).astype(BF)
            dks[i, :, 192 + HEAD * h : 256 + HEAD * h] = d_value.astype(BF)
        return carry

    lax.fori_loop(0, n, tile_step, 0)
    for i, ref in enumerate(d_keys):
        ref[...] = dks[2 * i : 2 * i + 2]
    if last:
        for j, ref in enumerate(d_queries):
            ref[...] = (dqs[j] * SCALE).astype(BF)


def tail_kernel(
    coords, order, table, tok, cot, lna, wqkv, ga, gm, dq0, dq1, dq2, dq3, dkv0, dkv1,
    att, d_ln_mlp, small_in, g0, g1, g2, g3, upstream, grads,
):
    d_query = (
        dq0[...].astype(F32) + dq1[...].astype(F32) + dq2[...].astype(F32) + dq3[...].astype(F32)
    ).T
    d_kv = dkv0[...].astype(F32) + dkv1[...].astype(F32)
    both = jnp.concatenate([d_query, d_kv[:, :192]], axis=1)
    cosine, left_sine, right_sine = spin_tables(coords, order, table)
    pieces = []
    for t in range(3):
        x = both[:, 128 * t : 128 * t + 128]
        back = (
            x * cosine
            + pltpu.roll(x * left_sine, 8, 1)
            + pltpu.roll(x * right_sine, 120, 1)
        )
        pieces += [back[:, :HEAD], back[:, HEAD:]]
    cols = []
    for h in range(HEADS):
        cols += [pieces[h], pieces[3 + h], d_kv[:, 192 + HEAD * h : 256 + HEAD * h]]
    d_joined = jnp.concatenate(cols, axis=1).astype(BF)
    turned = mm_tn(d_joined, lna[...]).astype(BF)
    for piece in range(3):
        grads[piece] = turned[192 * piece : 192 * piece + 192, :]
    grads[3] = mm_tn(att[...], cot[...]).astype(BF)
    for slot, ref in enumerate((g0, g1, g2, g3)):
        ref[0:192, :] = grads[(coords[2] + slot) % 4]
    d_attn = mm(d_joined, wqkv[...])
    d_mlp = d_ln_mlp[...]
    xhat, _ = normed(tok[...])
    upstream[...] = (d_attn * row(ga) + d_mlp * row(gm)).astype(BF)
    sums = [
        jnp.sum(v, axis=0, keepdims=True) for v in (d_attn * xhat, d_attn, d_mlp * xhat, d_mlp)
    ]
    bias = jnp.sum(d_joined.astype(F32), axis=0, keepdims=True)
    bias = jnp.concatenate([bias, jnp.zeros((1, 192), F32)], axis=1)
    small = jnp.concatenate([*sums, small_in[0:2, :], bias, jnp.zeros((9, 768), F32)], axis=0)
    for ref in (g0, g1, g2, g3):
        ref[192:208, :] = small.astype(BF)


def first_sum_kernel(coords, p0, p1, p2, p3, b0, b1, b2, b3, order, total):
    for slot, ref in enumerate((p0, p1, p2, p3)):
        order[(coords[2] + 4 - slot) % 4] = ref[...].astype(F32)
    rows = ((order[0] + order[1]) + (order[2] + order[3])).astype(BF)
    for block in range(4):
        total[block] = rows[48 * block : 48 * block + 48, :]
    for slot, ref in enumerate((b0, b1, b2, b3)):
        ref[0:48, :] = total[(coords[1] + slot) % 4]
        ref[48:64, :] = rows[192:208, :]


def second_sum_kernel(coords, b0, b1, b2, b3, out, order):
    for slot, ref in enumerate((b0, b1, b2, b3)):
        order[(coords[1] + 4 - slot) % 4] = ref[...].astype(F32)
    out[...] = ((order[0] + order[1]) + (order[2] + order[3])).astype(BF)


def token_kernel(tok, cot, e0, e1, out):
    xhat, rstd = normed(tok[...])
    e = e0[...].astype(F32) + e1[...].astype(F32)
    inner = e - jnp.mean(e, axis=-1, keepdims=True)
    inner = inner - xhat * jnp.mean(e * xhat, axis=-1, keepdims=True)
    out[...] = (cot[...].astype(F32) + rstd * inner).astype(BF)


def quarter_kernel(coords, b0, b1, b2, b3, out):
    for slot, ref in enumerate((b0, b1, b2, b3)):
        out[(coords[1] + slot) % 4] = ref[...]


def assemble_kernel(coords, p0, p1, p2, p3, gq, gd, whole):
    for slot, ref in enumerate((p0, p1, p2, p3)):
        whole[(coords[2] + slot) % 4] = ref[...].astype(F32)
    for block in range(12):
        gq[48 * block : 48 * block + 48, :] = whole[block // 4, block % 4]
    for block in range(4):
        gd[48 * block : 48 * block + 48, :] = whole[3, block]


def call(kernel, outs, args, scalars, scratch=(), mib=48, unread=0):
    smem = pl.BlockSpec(memory_space=pltpu.SMEM)
    vmem = pl.BlockSpec(memory_space=pltpu.VMEM)
    shapes = [jax.ShapeDtypeStruct(s, d) for s, d in outs]
    return pl.pallas_call(
        kernel,
        out_shape=shapes,
        in_specs=[smem] * scalars
        + [vmem] * (len(args) - scalars - unread)
        + [pl.BlockSpec(memory_space=pl.ANY)] * unread,
        out_specs=[vmem] * len(shapes),
        scratch_shapes=list(scratch),
        compiler_params=pltpu.CompilerParams(vmem_limit_bytes=mib << 20),
        cost_estimate=pl.CostEstimate(flops=0, bytes_accessed=1024, transcendentals=0),
    )(*args)


def hop(x, axis, step):
    n = lax.axis_size(axis)
    return lax.ppermute(x, axis, [(i, (i + step) % n) for i in range(n)])


def add(*parts):
    return functools.reduce(jnp.add, [p.astype(F32) for p in parts])


def on_device(
    tokens,
    block_order,
    cotangent,
    w_qkv,
    b_qkv,
    w_dense,
    b_dense,
    w_up,
    b_up,
    w_down,
    b_down,
    gain_attn,
    shift_attn,
    gain_mlp,
    shift_mlp,
):
    coords = jnp.stack([lax.axis_index(a) for a in CTX]).astype(jnp.int32)
    table = jnp.asarray(lane_table())
    w_turned = w_qkv.T

    qdo, kv, ln_attn, ln_mlp = call(
        front_kernel,
        [((256, 384), BF), ((256, 384), BF), ((256, 768), BF), ((256, 768), BF)],
        (coords, block_order, table, tokens, cotangent, w_turned, w_dense,
         gain_attn, shift_attn, gain_mlp, shift_mlp, b_qkv),
        2,
        mib=60,
    )
    kv_x = hop(kv, "xl", 1)
    down, up = hop(kv, "z", 1), hop(kv, "z", -1)
    down_x, up_x = hop(kv_x, "z", 1), hop(kv_x, "z", -1)
    kvs = [kv, kv_x, up, up_x, hop(down, "z", 1), hop(up_x, "z", -1), down, down_x]
    qdos = [qdo] + [hop(qdo, "y", -j) for j in (1, 2, 3)]

    grads_mlp, small_mlp, part_mlp, d_ln_mlp = call(
        mlp_kernel,
        [((1536, 768), BF), ((8, 768), F32), ((256, 768), F32), ((256, 768), F32)],
        (ln_mlp, cotangent, w_up, b_up, w_down, kv_x),
        0,
        unread=1,
    )
    grads_mlp = lax.psum_scatter(grads_mlp, ("z", "y"), scatter_dimension=0, tiled=True)
    *outs, stats = call(
        forward_kernel,
        [((192, 256), BF)] * 4 + [((4, 8, 256), F32)],
        (coords, block_order, *qdos, *kvs),
        2,
        scratch=[pltpu.VMEM((4, 256, 384), BF), pltpu.VMEM((4, 192, 256), BF)],
    )
    stats_all = [stats] + [hop(stats, "y", -j) for j in (1, 2, 3)]
    outs = [outs[0]] + [hop(outs[j], "y", j) for j in (1, 2, 3)]
    att, branch = call(
        merge_kernel,
        [((256, 192), BF), ((256, 768), BF)],
        (*stats_all, *outs, w_dense, part_mlp),
        0,
    )
    branch = add(branch, hop(branch, "c", 1)).astype(BF)
    branch = add(branch, hop(branch, "xh", 1))
    output = (tokens.astype(F32) + branch + b_dense + b_down).astype(BF)

    def backward(tiles, stats_in, before, last, after=()):
        first = before is None
        n = len(tiles)
        kept = [((4, 8, 256), F32)] if first else []
        d_out = [((192, 256), BF)] * 4 if last else [((4, 192, 256), F32)]
        scratch = [pltpu.VMEM((n, 256, 384), BF)] * 2
        if last:
            scratch.append(pltpu.VMEM((4, 192, 256), F32))
        return call(
            functools.partial(backward_kernel, tiles, first, last, len(after)),
            kept + [((2, 256, 384), BF)] * (n // 2) + d_out,
            (coords, block_order, *stats_in, *qdos, *[kvs[t] for t in tiles])
            + (() if first else (before,))
            + tuple(after),
            2,
            unread=len(after),
            scratch=scratch,
        )

    whole, d_far, d_q = backward((4, 5), stats_all, None, False)
    far = hop(d_far, "z", 2)
    d_up, d_down, d_q = backward((2, 3, 6, 7), [whole], d_q, False)
    near = [hop(d_up, "z", 1), hop(d_down, "z", -1)]
    d_kv, *d_qs = backward((0, 1), [whole], d_q, True, (far,))
    (grads_mlp,) = call(
        keep_kernel, [(grads_mlp.shape, BF)], (grads_mlp, d_kv), 0, unread=1
    )
    grads_mlp = add(grads_mlp, hop(grads_mlp, "xl", 1)).astype(BF)
    grads_mlp = lax.all_gather(grads_mlp, ("z", "y"), axis=0, tiled=True)
    d_queries = [d_qs[0]] + [hop(d_qs[j], "y", j) for j in (1, 2, 3)]
    d_kv_other = hop(add(d_kv[1], far[1], near[0][1], near[1][1]).astype(BF), "xl", 1)
    d_kv_own = add(d_kv[0], far[0], near[0][0], near[1][0]).astype(BF)
    *pieces, upstream = call(
        tail_kernel,
        [((208, 768), BF)] * 4 + [((256, 768), BF)],
        (coords, block_order, table, tokens, cotangent, ln_attn, w_turned, gain_attn, gain_mlp,
         *d_queries, d_kv_own, d_kv_other, att, d_ln_mlp, small_mlp),
        2,
        scratch=[pltpu.VMEM((4, 192, 768), BF)],
    )

    pieces = [pieces[0]] + [hop(pieces[j], "y", j) for j in (1, 2, 3)]
    upstream = add(upstream, hop(upstream, "c", 1)).astype(BF)
    upstream_far = hop(upstream, "xh", 1)
    blocks = call(
        first_sum_kernel,
        [((64, 768), BF)] * 4,
        (coords, *pieces),
        1,
        scratch=[pltpu.VMEM((4, 208, 768), F32), pltpu.VMEM((4, 48, 768), BF)],
    )
    (block,) = call(
        second_sum_kernel,
        [((64, 768), BF)],
        (coords, blocks[0], *[hop(blocks[j], "z", j) for j in (1, 2, 3)]),
        1,
        scratch=[pltpu.VMEM((4, 64, 768), F32)],
    )
    block = add(block, hop(block, "xl", 1))
    small = block[48:56]
    gains = small + hop(small, "c", 1)
    gains = gains + hop(gains, "xh", 1)
    block = block[0:48].astype(BF)
    (quarter,) = call(
        quarter_kernel,
        [((4, 48, 768), BF)],
        (coords, block, *[hop(block, "z", -j) for j in (1, 2, 3)]),
        1,
    )
    grad_turned, grad_w_dense = call(
        assemble_kernel,
        [((576, 768), F32), ((192, 768), F32)],
        (coords, quarter, *[hop(quarter, "y", -j) for j in (1, 2, 3)]),
        1,
        scratch=[pltpu.VMEM((4, 4, 48, 768), F32)],
    )
    (grad_tokens,) = call(
        token_kernel, [((256, 768), BF)], (tokens, cotangent, upstream, upstream_far), 0
    )

    grad_w_up, grad_w_down = call(
        widen_kernel, [((768, 768), F32)] * 2, (grads_mlp, quarter), 0, unread=1
    )
    return (
        output,
        grad_tokens,
        grad_turned.T,
        small[6, :576],
        grad_w_dense,
        small[5],
        grad_w_up,
        small[4],
        grad_w_down,
        small[5],
        gains[0],
        gains[1],
        gains[2],
        gains[3],
    )


def solution(mesh):
    fine = Mesh(mesh.devices.reshape(2, 4, 4, 2, 2), CTX + TP)
    rows, cols = P(CTX, None), P(None, TP)
    return jax.shard_map(
        on_device,
        mesh=fine,
        in_specs=(
            rows, P(), rows, cols, P(TP), P(TP, None), P(), cols, P(TP), P(TP, None),
            P(), P(), P(), P(), P(),
        ),
        out_specs=(
            rows, rows, cols, P(TP), P(TP, None), P(), cols, P(TP), P(TP, None),
            P(), P(), P(), P(), P(),
        ),
        check_vma=False,
    )
```

```python
import functools
import math

import jax
import jax.numpy as jnp
import numpy as np
from jax import lax
from jax.experimental import pallas as pl
from jax.experimental.pallas import tpu as pltpu
from jax.sharding import Mesh
from jax.sharding import PartitionSpec as P

HEAD = 64
ROT = 16
HEADS = 3
EPSILON = 1e-05
MASKED = -1e30
CTX = ("xl", "z", "y")
TP = ("xh", "c")
F32 = jnp.float32
BF = jnp.bfloat16
LOG2E = math.log2(math.e)
SCALE = 1.0 / math.sqrt(HEAD)
SCORE = SCALE * LOG2E
NT = (((1,), (1,)), ((), ()))
TN = (((0,), (0,)), ((), ()))


def mm(a, b):
    return jnp.dot(a, b, preferred_element_type=F32)


def mm_nt(a, b):
    return lax.dot_general(a, b, NT, preferred_element_type=F32)


def mm_tn(a, b):
    return lax.dot_general(a, b, TN, preferred_element_type=F32)


def lane_table():
    lane = np.arange(128) % HEAD
    table = np.zeros((8, 128), np.float32)
    table[0] = np.where(lane < ROT, 10000.0 ** (-2.0 * (lane % 8) / ROT), 0.0)
    table[1] = lane < 8
    table[2] = (lane >= 8) & (lane < ROT)
    return table


def spin_tables(coords, order, table):
    shard = (coords[0] * 4 + coords[1]) * 4 + coords[2]
    step = lax.broadcasted_iota(jnp.int32, (128, 128), 0)
    places = jnp.concatenate(
        [step + order[2 * shard] * 128, step + order[2 * shard + 1] * 128], axis=0
    )
    angles = places.astype(F32) * table[0:1, :]
    sine = jnp.sin(angles)
    return jnp.cos(angles), sine * -table[1:2, :], sine * table[2:3, :]


def row(ref):
    return ref[...].reshape(1, -1)


def keep_kernel(x, *refs):
    refs[-1][...] = x[...]


def widen_kernel(x, after, up, down):
    up[...] = x[0:768, :].astype(F32)
    down[...] = x[768:1536, :].astype(F32)


def normed(tokens):
    values = tokens.astype(F32)
    centred = values - jnp.mean(values, axis=-1, keepdims=True)
    rstd = lax.rsqrt(jnp.mean(centred * centred, axis=-1, keepdims=True) + EPSILON)
    return centred * rstd, rstd


def front_kernel(
    coords, order, table, tok, cot, wqkv, wd, ga, sa, gm, sm, bqkv, qdo, kv, lna, lnm
):
    xhat, _ = normed(tok[...])
    ln = (xhat * row(ga) + row(sa)).astype(BF)
    lna[...] = ln
    lnm[...] = (xhat * row(gm) + row(sm)).astype(BF)
    joined = mm_nt(ln, wqkv[...]) + row(bqkv)
    cosine, left_sine, right_sine = spin_tables(coords, order, table)
    half = lax.broadcasted_iota(jnp.int32, (256, 128), 1) < HEAD
    tiles = []
    for t in range(4):
        x = joined[:, 128 * t : 128 * t + 128]
        spun = (
            x * cosine + pltpu.roll(x, 120, 1) * left_sine + pltpu.roll(x, 8, 1) * right_sine
        )
        if t == 1:
            spun = jnp.where(half, x, spun)
        if t == 2:
            spun = jnp.where(half, spun, x)
        tiles.append(spun)
    pieces = []
    for t in range(4):
        pieces += [tiles[t][:, :HEAD], tiles[t][:, HEAD:]]
    pieces.append(joined[:, 512:576])
    d_att = mm_nt(cot[...], wd[...])
    qdo[...] = jnp.concatenate(
        [pieces[0], pieces[3], pieces[6], d_att], axis=1
    ).astype(BF)
    kv[...] = jnp.concatenate([pieces[i] for i in (1, 4, 7, 2, 5, 8)], axis=1).astype(BF)


def mlp_kernel(ln, cot, wu, bu, wdn, *refs):
    gw, small, part, d_ln = refs[-4:]
    up = mm(ln[...], wu[...]) + row(bu)
    phi = 0.5 * (1.0 + lax.erf(up * math.sqrt(0.5)))
    hid = (up * phi).astype(BF)
    slope = phi + up * (jnp.exp(up * up * -0.5) * (1.0 / math.sqrt(2.0 * math.pi)))
    d_up = (mm_nt(cot[...], wdn[...]) * slope).astype(BF)
    gw[0:768, :] = mm_tn(ln[...], d_up).astype(BF)
    gw[768:1536, :] = mm_tn(hid, cot[...]).astype(BF)
    part[...] = mm(hid, wdn[...])
    d_ln[...] = mm_nt(d_up, wu[...])
    small[0:1, :] = jnp.sum(d_up.astype(F32), axis=0, keepdims=True)
    small[1:2, :] = jnp.sum(cot[...].astype(F32), axis=0, keepdims=True)
    small[2:8, :] = jnp.zeros((6, 768), F32)


def mask_tile(scores, gap, q_places, k_places):
    rows = []
    for kb in range(2):
        cells = []
        for qb in range(2):
            cell = scores[128 * kb : 128 * kb + 128, 128 * qb : 128 * qb + 128]
            cells.append(jnp.where(gap <= (q_places[qb] - k_places[kb]) * 128, cell, MASKED))
        rows.append(jnp.concatenate(cells, axis=1))
    return jnp.concatenate(rows, axis=0)


def gap_table():
    return lax.broadcasted_iota(jnp.int32, (128, 128), 0) - lax.broadcasted_iota(
        jnp.int32, (128, 128), 1
    )


def query_places(coords, order, slot):
    shard = (coords[0] * 4 + coords[1]) * 4 + (coords[2] + slot) % 4
    return order[2 * shard], order[2 * shard + 1]


def key_places(coords, order, tile):
    shard = ((coords[0] + tile % 2) % 2 * 4 + (coords[1] + tile // 2) % 4) * 4 + coords[2]
    return order[2 * shard], order[2 * shard + 1]


def forward_kernel(coords, order, *refs):
    queries, keys = refs[0:4], refs[4:12]
    outs, stats, qs, os = refs[12:16], refs[16], refs[17], refs[18]
    for j, ref in enumerate(queries):
        qs[j] = ref[...]
    gap = gap_table()

    def slot_step(j, carry):
        q_places = query_places(coords, order, j)
        for h in range(HEADS):
            query = qs[j, :, HEAD * h : HEAD * h + HEAD]
            d_att = qs[j, :, 192 + HEAD * h : 256 + HEAD * h]
            tiles, tops = [], []
            for t in range(8):
                key = keys[t][:, HEAD * h : HEAD * h + HEAD]
                scores = mask_tile(
                    mm_nt(key, query), gap, q_places, key_places(coords, order, t)
                )
                tiles.append(scores)
                tops.append(jnp.max(scores, axis=0, keepdims=True))
            top = functools.reduce(jnp.maximum, tops) * SCORE
            total = jnp.zeros((1, 256), F32)
            out = jnp.zeros((HEAD, 256), F32)
            for t in range(8):
                weights = jnp.exp2(tiles[t] * SCORE - top)
                total = total + jnp.sum(weights, axis=0, keepdims=True)
                value = keys[t][:, 192 + HEAD * h : 256 + HEAD * h]
                out = out + mm(value.T, weights.astype(BF))
            out = out / total
            os[j, HEAD * h : HEAD * h + HEAD, :] = out.astype(BF)
            stats[j, h : h + 1, :] = top + jnp.log2(total)
            stats[j, 3 + h : 4 + h, :] = jnp.sum(
                d_att.astype(F32).T * out, axis=0, keepdims=True
            )
        stats[j, 6:8, :] = jnp.zeros((2, 256), F32)
        return carry

    lax.fori_loop(0, 4, slot_step, 0)
    for j, ref in enumerate(outs):
        ref[...] = os[j]


def merge_kernel(s0, s1, s2, s3, o0, o1, o2, o3, wd, part, att, branch):
    stats = [ref[-step % 4] for step, ref in enumerate((s0, s1, s2, s3))]
    outs = [o0, o3, o2, o1]
    rows = []
    for h in range(HEADS):
        logs = [s[h : h + 1, :] for s in stats]
        top = functools.reduce(jnp.maximum, logs)
        shares = [jnp.exp2(v - top) for v in logs]
        total = functools.reduce(jnp.add, shares)
        mixed = functools.reduce(
            jnp.add,
            [
                share * ref[HEAD * h : HEAD * h + HEAD, :].astype(F32)
                for share, ref in zip(shares, outs, strict=True)
            ],
        )
        rows.append(mixed / total)
    att_low = jnp.concatenate(rows, axis=0).T.astype(BF)
    att[...] = att_low
    branch[...] = (mm(att_low, wd[...]) + part[...]).astype(BF)


def backward_kernel(tiles, first, last, unread, coords, order, *refs):
    n = len(tiles)
    refs = list(refs)

    def take(count):
        taken = refs[:count]
        del refs[:count]
        return taken

    stats = take(4 if first else 1)
    queries, keys = take(4), take(n)
    d_before = None if first else take(1)[0]
    take(unread)
    if first:
        (st,) = take(1)
    else:
        (st,) = stats
    d_keys = take(n // 2)
    d_queries = take(4 if last else 1)
    ks, dks = take(2)
    dqs = take(1)[0] if last else d_queries[0]
    for i, ref in enumerate(keys):
        ks[i] = ref[...]
    dqs[...] = jnp.zeros_like(dqs) if first else d_before[...]
    for j in range(4 if first else 0):
        parts = [ref[(j - step) % 4] for step, ref in enumerate(stats)]
        logs = [p[0:3, :] for p in parts]
        top = functools.reduce(jnp.maximum, logs)
        total = functools.reduce(jnp.add, [jnp.exp2(v - top) for v in logs])
        whole = top + jnp.log2(total)
        st[j, 0:3, :] = whole
        st[j, 3:6, :] = functools.reduce(
            jnp.add, [jnp.exp2(p[0:3, :] - whole) * p[3:6, :] for p in parts]
        )
        st[j, 6:8, :] = jnp.zeros((2, 256), F32)
    gap = gap_table()

    def tile_step(i, carry):
        step = tiles[2] - tiles[0] if n > 2 else 0
        k_places = key_places(coords, order, tiles[0] + i % 2 + i // 2 * step)
        for h in range(HEADS):
            key = ks[i, :, HEAD * h : HEAD * h + HEAD]
            value = ks[i, :, 192 + HEAD * h : 256 + HEAD * h]
            key_turned = key.T
            d_key = jnp.zeros((256, HEAD), F32)
            d_value = jnp.zeros((256, HEAD), F32)
            for j in range(4):
                query = queries[j][:, HEAD * h : HEAD * h + HEAD]
                d_att = queries[j][:, 192 + HEAD * h : 256 + HEAD * h]
                scores = mask_tile(
                    mm_nt(key, query), gap, query_places(coords, order, j), k_places
                )
                weights = jnp.exp2(scores * SCORE - st[j, h : h + 1, :])
                d_weights = mm_nt(value, d_att)
                d_scores = (weights * (d_weights - st[j, 3 + h : 4 + h, :])).astype(BF)
                d_value = d_value + mm(weights.astype(BF), d_att)
                d_key = d_key + mm(d_scores, query)
                dqs[j, HEAD * h : HEAD * h + HEAD, :] += mm(key_turned, d_scores)
            dks[i, :, HEAD * h : HEAD * h + HEAD] = (d_key * SCALE).astype(BF)
            dks[i, :, 192 + HEAD * h : 256 + HEAD * h] = d_value.astype(BF)
        return carry

    lax.fori_loop(0, n, tile_step, 0)
    for i, ref in enumerate(d_keys):
        ref[...] = dks[2 * i : 2 * i + 2]
    if last:
        for j, ref in enumerate(d_queries):
            ref[...] = (dqs[j] * SCALE).astype(BF)


def tail_kernel(
    coords, order, table, tok, cot, lna, wqkv, ga, gm, dq0, dq1, dq2, dq3, dkv0, dkv1,
    att, d_ln_mlp, small_in, g0, g1, g2, g3, upstream, grads,
):
    d_query = (
        dq0[...].astype(F32) + dq1[...].astype(F32) + dq2[...].astype(F32) + dq3[...].astype(F32)
    ).T
    d_kv = dkv0[...].astype(F32) + dkv1[...].astype(F32)
    both = jnp.concatenate([d_query, d_kv[:, :192]], axis=1)
    cosine, left_sine, right_sine = spin_tables(coords, order, table)
    pieces = []
    for t in range(3):
        x = both[:, 128 * t : 128 * t + 128]
        back = (
            x * cosine
            + pltpu.roll(x * left_sine, 8, 1)
            + pltpu.roll(x * right_sine, 120, 1)
        )
        pieces += [back[:, :HEAD], back[:, HEAD:]]
    cols = []
    for h in range(HEADS):
        cols += [pieces[h], pieces[3 + h], d_kv[:, 192 + HEAD * h : 256 + HEAD * h]]
    d_joined = jnp.concatenate(cols, axis=1).astype(BF)
    turned = mm_tn(d_joined, lna[...]).astype(BF)
    for piece in range(3):
        grads[piece] = turned[192 * piece : 192 * piece + 192, :]
    grads[3] = mm_tn(att[...], cot[...]).astype(BF)
    for slot, ref in enumerate((g0, g1, g2, g3)):
        ref[0:192, :] = grads[(coords[2] + slot) % 4]
    d_attn = mm(d_joined, wqkv[...])
    d_mlp = d_ln_mlp[...]
    xhat, _ = normed(tok[...])
    upstream[...] = (d_attn * row(ga) + d_mlp * row(gm)).astype(BF)
    sums = [
        jnp.sum(v, axis=0, keepdims=True) for v in (d_attn * xhat, d_attn, d_mlp * xhat, d_mlp)
    ]
    bias = jnp.sum(d_joined.astype(F32), axis=0, keepdims=True)
    bias = jnp.concatenate([bias, jnp.zeros((1, 192), F32)], axis=1)
    small = jnp.concatenate([*sums, small_in[0:2, :], bias, jnp.zeros((9, 768), F32)], axis=0)
    for ref in (g0, g1, g2, g3):
        ref[192:208, :] = small.astype(BF)


def first_sum_kernel(coords, p0, p1, p2, p3, b0, b1, b2, b3, order, total):
    for slot, ref in enumerate((p0, p1, p2, p3)):
        order[(coords[2] + 4 - slot) % 4] = ref[...].astype(F32)
    rows = ((order[0] + order[1]) + (order[2] + order[3])).astype(BF)
    for block in range(4):
        total[block] = rows[48 * block : 48 * block + 48, :]
    for slot, ref in enumerate((b0, b1, b2, b3)):
        ref[0:48, :] = total[(coords[1] + slot) % 4]
        ref[48:64, :] = rows[192:208, :]


def second_sum_kernel(coords, b0, b1, b2, b3, out, order):
    for slot, ref in enumerate((b0, b1, b2, b3)):
        order[(coords[1] + 4 - slot) % 4] = ref[...].astype(F32)
    out[...] = ((order[0] + order[1]) + (order[2] + order[3])).astype(BF)


def token_kernel(tok, cot, e0, e1, out):
    xhat, rstd = normed(tok[...])
    e = e0[...].astype(F32) + e1[...].astype(F32)
    inner = e - jnp.mean(e, axis=-1, keepdims=True)
    inner = inner - xhat * jnp.mean(e * xhat, axis=-1, keepdims=True)
    out[...] = (cot[...].astype(F32) + rstd * inner).astype(BF)


def quarter_kernel(coords, b0, b1, b2, b3, out):
    for slot, ref in enumerate((b0, b1, b2, b3)):
        out[(coords[1] + slot) % 4] = ref[...]


def assemble_kernel(coords, p0, p1, p2, p3, after, gq, gd, whole):
    for slot, ref in enumerate((p0, p1, p2, p3)):
        whole[(coords[2] + slot) % 4] = ref[...].astype(F32)
    for block in range(12):
        gq[48 * block : 48 * block + 48, :] = whole[block // 4, block % 4]
    for block in range(4):
        gd[48 * block : 48 * block + 48, :] = whole[3, block]


def call(kernel, outs, args, scalars, scratch=(), mib=48, unread=0):
    smem = pl.BlockSpec(memory_space=pltpu.SMEM)
    vmem = pl.BlockSpec(memory_space=pltpu.VMEM)
    shapes = [jax.ShapeDtypeStruct(s, d) for s, d in outs]
    return pl.pallas_call(
        kernel,
        out_shape=shapes,
        in_specs=[smem] * scalars
        + [vmem] * (len(args) - scalars - unread)
        + [pl.BlockSpec(memory_space=pl.ANY)] * unread,
        out_specs=[vmem] * len(shapes),
        scratch_shapes=list(scratch),
        compiler_params=pltpu.CompilerParams(vmem_limit_bytes=mib << 20),
        cost_estimate=pl.CostEstimate(flops=0, bytes_accessed=1024, transcendentals=0),
    )(*args)


def hop(x, axis, step):
    n = lax.axis_size(axis)
    return lax.ppermute(x, axis, [(i, (i + step) % n) for i in range(n)])


def add(*parts):
    return functools.reduce(jnp.add, [p.astype(F32) for p in parts])


def on_device(
    tokens,
    block_order,
    cotangent,
    w_qkv,
    b_qkv,
    w_dense,
    b_dense,
    w_up,
    b_up,
    w_down,
    b_down,
    gain_attn,
    shift_attn,
    gain_mlp,
    shift_mlp,
):
    coords = jnp.stack([lax.axis_index(a) for a in CTX]).astype(jnp.int32)
    table = jnp.asarray(lane_table())
    w_turned = w_qkv.T

    qdo, kv, ln_attn, ln_mlp = call(
        front_kernel,
        [((256, 384), BF), ((256, 384), BF), ((256, 768), BF), ((256, 768), BF)],
        (coords, block_order, table, tokens, cotangent, w_turned, w_dense,
         gain_attn, shift_attn, gain_mlp, shift_mlp, b_qkv),
        2,
        mib=60,
    )
    kv_x = hop(kv, "xl", 1)
    down, up = hop(kv, "z", 1), hop(kv, "z", -1)
    down_x, up_x = hop(kv_x, "z", 1), hop(kv_x, "z", -1)
    kvs = [kv, kv_x, up, up_x, hop(down, "z", 1), hop(up_x, "z", -1), down, down_x]
    qdos = [qdo] + [hop(qdo, "y", -j) for j in (1, 2, 3)]

    grads_mlp, small_mlp, part_mlp, d_ln_mlp = call(
        mlp_kernel,
        [((1536, 768), BF), ((8, 768), F32), ((256, 768), F32), ((256, 768), F32)],
        (ln_mlp, cotangent, w_up, b_up, w_down, up_x, down, down_x, *qdos[1:]),
        0,
        unread=6,
    )
    grads_mlp = lax.psum_scatter(grads_mlp, ("z", "y"), scatter_dimension=0, tiled=True)
    *outs, stats = call(
        forward_kernel,
        [((192, 256), BF)] * 4 + [((4, 8, 256), F32)],
        (coords, block_order, *qdos, *kvs),
        2,
        scratch=[pltpu.VMEM((4, 256, 384), BF), pltpu.VMEM((4, 192, 256), BF)],
    )
    stats_all = [stats] + [hop(stats, "y", -j) for j in (1, 2, 3)]
    outs = [outs[0]] + [hop(outs[j], "y", j) for j in (1, 2, 3)]
    att, branch = call(
        merge_kernel,
        [((256, 192), BF), ((256, 768), BF)],
        (*stats_all, *outs, w_dense, part_mlp),
        0,
    )
    branch_near = hop(branch, "c", 1)
    branch = add(branch, branch_near).astype(BF)
    branch = add(branch, hop(branch, "xh", 1))
    output = (tokens.astype(F32) + branch + b_dense + b_down).astype(BF)

    def backward(tiles, stats_in, before, last, after=()):
        first = before is None
        n = len(tiles)
        kept = [((4, 8, 256), F32)] if first else []
        d_out = [((192, 256), BF)] * 4 if last else [((4, 192, 256), F32)]
        scratch = [pltpu.VMEM((n, 256, 384), BF)] * 2
        if last:
            scratch.append(pltpu.VMEM((4, 192, 256), F32))
        return call(
            functools.partial(backward_kernel, tiles, first, last, len(after)),
            kept + [((2, 256, 384), BF)] * (n // 2) + d_out,
            (coords, block_order, *stats_in, *qdos, *[kvs[t] for t in tiles])
            + (() if first else (before,))
            + tuple(after),
            2,
            unread=len(after),
            scratch=scratch,
        )

    whole, d_far, d_q = backward((4, 5), stats_all, None, False)
    far = hop(d_far, "z", 2)
    d_up, d_down, d_q = backward((2, 3, 6, 7), [whole], d_q, False)
    near = [hop(d_up, "z", 1), hop(d_down, "z", -1)]
    d_kv, *d_qs = backward((0, 1), [whole], d_q, True, (far, branch_near))
    d_queries = [d_qs[0]] + [hop(d_qs[j], "y", j) for j in (1, 2, 3)]
    d_kv_send = add(d_kv[1], far[1], near[0][1], near[1][1]).astype(BF)
    d_kv_other = hop(d_kv_send, "xl", 1)
    d_kv_own = add(d_kv[0], far[0], near[0][0], near[1][0]).astype(BF)
    (grads_mlp,) = call(
        keep_kernel, [(grads_mlp.shape, BF)], (grads_mlp, d_kv_send, *d_queries[1:]), 0, unread=4
    )
    grads_mlp = add(grads_mlp, hop(grads_mlp, "xl", 1)).astype(BF)
    grads_mlp = lax.all_gather(grads_mlp, ("z", "y"), axis=0, tiled=True)
    *pieces, upstream = call(
        tail_kernel,
        [((208, 768), BF)] * 4 + [((256, 768), BF)],
        (coords, block_order, table, tokens, cotangent, ln_attn, w_turned, gain_attn, gain_mlp,
         *d_queries, d_kv_own, d_kv_other, att, d_ln_mlp, small_mlp),
        2,
        scratch=[pltpu.VMEM((4, 192, 768), BF)],
    )

    pieces = [pieces[0]] + [hop(pieces[j], "y", j) for j in (1, 2, 3)]
    upstream = add(upstream, hop(upstream, "c", 1)).astype(BF)
    upstream_far = hop(upstream, "xh", 1)
    blocks = call(
        first_sum_kernel,
        [((64, 768), BF)] * 4,
        (coords, *pieces),
        1,
        scratch=[pltpu.VMEM((4, 208, 768), F32), pltpu.VMEM((4, 48, 768), BF)],
    )
    (block,) = call(
        second_sum_kernel,
        [((64, 768), BF)],
        (coords, blocks[0], *[hop(blocks[j], "z", j) for j in (1, 2, 3)]),
        1,
        scratch=[pltpu.VMEM((4, 64, 768), F32)],
    )
    block = add(block, hop(block, "xl", 1))
    small = block[48:56]
    gains = small + hop(small, "c", 1)
    gains = gains + hop(gains, "xh", 1)
    block = block[0:48].astype(BF)
    (quarter,) = call(
        quarter_kernel,
        [((4, 48, 768), BF)],
        (coords, block, *[hop(block, "z", -j) for j in (1, 2, 3)]),
        1,
    )
    grad_w_up, grad_w_down = call(
        widen_kernel, [((768, 768), F32)] * 2, (grads_mlp, quarter), 0, unread=1
    )
    grad_turned, grad_w_dense = call(
        assemble_kernel,
        [((576, 768), F32), ((192, 768), F32)],
        (coords, quarter, *[hop(quarter, "y", -j) for j in (1, 2, 3)], grad_w_up),
        1,
        unread=1,
        scratch=[pltpu.VMEM((4, 4, 48, 768), F32)],
    )
    (grad_tokens,) = call(
        token_kernel, [((256, 768), BF)], (tokens, cotangent, upstream, upstream_far), 0
    )

    return (
        output,
        grad_tokens,
        grad_turned.T,
        small[6, :576],
        grad_w_dense,
        small[5],
        grad_w_up,
        small[4],
        grad_w_down,
        small[5],
        gains[0],
        gains[1],
        gains[2],
        gains[3],
    )


def solution(mesh):
    fine = Mesh(mesh.devices.reshape(2, 4, 4, 2, 2), CTX + TP)
    rows, cols = P(CTX, None), P(None, TP)
    return jax.shard_map(
        on_device,
        mesh=fine,
        in_specs=(
            rows, P(), rows, cols, P(TP), P(TP, None), P(), cols, P(TP), P(TP, None),
            P(), P(), P(), P(), P(),
        ),
        out_specs=(
            rows, rows, cols, P(TP), P(TP, None), P(), cols, P(TP), P(TP, None),
            P(), P(), P(), P(), P(),
        ),
        check_vma=False,
    )
```

```python
import functools
import math

import jax
import jax.numpy as jnp
import numpy as np
from jax import lax
from jax.experimental import pallas as pl
from jax.experimental.pallas import tpu as pltpu
from jax.sharding import Mesh
from jax.sharding import PartitionSpec as P

HEAD = 64
ROT = 16
HEADS = 3
EPSILON = 1e-05
MASKED = -1e30
CTX = ("xl", "z", "y")
TP = ("xh", "c")
F32 = jnp.float32
BF = jnp.bfloat16
LOG2E = math.log2(math.e)
SCALE = 1.0 / math.sqrt(HEAD)
SCORE = SCALE * LOG2E
NT = (((1,), (1,)), ((), ()))
TN = (((0,), (0,)), ((), ()))


def mm(a, b):
    return jnp.dot(a, b, preferred_element_type=F32)


def mm_nt(a, b):
    return lax.dot_general(a, b, NT, preferred_element_type=F32)


def mm_tn(a, b):
    return lax.dot_general(a, b, TN, preferred_element_type=F32)


def lane_table():
    lane = np.arange(128) % HEAD
    table = np.zeros((8, 128), np.float32)
    table[0] = np.where(lane < ROT, 10000.0 ** (-2.0 * (lane % 8) / ROT), 0.0)
    table[1] = lane < 8
    table[2] = (lane >= 8) & (lane < ROT)
    return table


def spin_tables(coords, order, table):
    shard = (coords[0] * 4 + coords[1]) * 4 + coords[2]
    step = lax.broadcasted_iota(jnp.int32, (128, 128), 0)
    places = jnp.concatenate(
        [step + order[2 * shard] * 128, step + order[2 * shard + 1] * 128], axis=0
    )
    angles = places.astype(F32) * table[0:1, :]
    sine = jnp.sin(angles)
    return jnp.cos(angles), sine * -table[1:2, :], sine * table[2:3, :]


def row(ref):
    return ref[...].reshape(1, -1)


def normed(tokens):
    values = tokens.astype(F32)
    centred = values - jnp.mean(values, axis=-1, keepdims=True)
    rstd = lax.rsqrt(jnp.mean(centred * centred, axis=-1, keepdims=True) + EPSILON)
    return centred * rstd, rstd


def front_kernel(
    coords, order, table, tok, cot, wqkv, wd, ga, sa, gm, sm, bqkv, wu, bu, wdn,
    qdo, kv, lna, gw, small, part, d_ln,
):
    xhat, _ = normed(tok[...])
    ln = (xhat * row(ga) + row(sa)).astype(BF)
    lna[...] = ln
    joined = mm_nt(ln, wqkv[...]) + row(bqkv)
    cosine, left_sine, right_sine = spin_tables(coords, order, table)
    half = lax.broadcasted_iota(jnp.int32, (256, 128), 1) < HEAD
    tiles = []
    for t in range(4):
        x = joined[:, 128 * t : 128 * t + 128]
        spun = (
            x * cosine + pltpu.roll(x, 120, 1) * left_sine + pltpu.roll(x, 8, 1) * right_sine
        )
        if t == 1:
            spun = jnp.where(half, x, spun)
        if t == 2:
            spun = jnp.where(half, spun, x)
        tiles.append(spun)
    pieces = []
    for t in range(4):
        pieces += [tiles[t][:, :HEAD], tiles[t][:, HEAD:]]
    pieces.append(joined[:, 512:576])
    d_att = mm_nt(cot[...], wd[...])
    qdo[...] = jnp.concatenate(
        [pieces[0], pieces[3], pieces[6], d_att], axis=1
    ).astype(BF)
    kv[...] = jnp.concatenate([pieces[i] for i in (1, 4, 7, 2, 5, 8)], axis=1).astype(BF)

    ln = (xhat * row(gm) + row(sm)).astype(BF)
    up = mm(ln, wu[...]) + row(bu)
    phi = 0.5 * (1.0 + lax.erf(up * math.sqrt(0.5)))
    hid = (up * phi).astype(BF)
    slope = phi + up * (jnp.exp(up * up * -0.5) * (1.0 / math.sqrt(2.0 * math.pi)))
    d_up = (mm_nt(cot[...], wdn[...]) * slope).astype(BF)
    gw[0:768, :] = mm_tn(ln, d_up).astype(BF)
    gw[768:1536, :] = mm_tn(hid, cot[...]).astype(BF)
    part[...] = mm(hid, wdn[...])
    d_ln[...] = mm_nt(d_up, wu[...])
    small[0:1, :] = jnp.sum(d_up.astype(F32), axis=0, keepdims=True)
    small[1:2, :] = jnp.sum(cot[...].astype(F32), axis=0, keepdims=True)
    small[2:8, :] = jnp.zeros((6, 768), F32)


def mask_tile(scores, gap, q_places, k_places):
    rows = []
    for kb in range(2):
        cells = []
        for qb in range(2):
            cell = scores[128 * kb : 128 * kb + 128, 128 * qb : 128 * qb + 128]
            cells.append(jnp.where(gap <= (q_places[qb] - k_places[kb]) * 128, cell, MASKED))
        rows.append(jnp.concatenate(cells, axis=1))
    return jnp.concatenate(rows, axis=0)


def gap_table():
    return lax.broadcasted_iota(jnp.int32, (128, 128), 0) - lax.broadcasted_iota(
        jnp.int32, (128, 128), 1
    )


def query_places(coords, order, slot):
    shard = (coords[0] * 4 + coords[1]) * 4 + (coords[2] + slot) % 4
    return order[2 * shard], order[2 * shard + 1]


def key_places(coords, order, tile):
    shard = ((coords[0] + tile % 2) % 2 * 4 + (coords[1] + tile // 2) % 4) * 4 + coords[2]
    return order[2 * shard], order[2 * shard + 1]


def forward_kernel(coords, order, *refs):
    queries, keys = refs[0:4], refs[4:12]
    outs, stats, qs, os = refs[12:16], refs[16], refs[17], refs[18]
    for j, ref in enumerate(queries):
        qs[j] = ref[...]
    gap = gap_table()

    def slot_step(j, carry):
        q_places = query_places(coords, order, j)
        for h in range(HEADS):
            query = qs[j, :, HEAD * h : HEAD * h + HEAD]
            d_att = qs[j, :, 192 + HEAD * h : 256 + HEAD * h]
            tiles, tops = [], []
            for t in range(8):
                key = keys[t][:, HEAD * h : HEAD * h + HEAD]
                scores = mask_tile(
                    mm_nt(key, query), gap, q_places, key_places(coords, order, t)
                )
                tiles.append(scores)
                tops.append(jnp.max(scores, axis=0, keepdims=True))
            top = functools.reduce(jnp.maximum, tops) * SCORE
            total = jnp.zeros((1, 256), F32)
            out = jnp.zeros((HEAD, 256), F32)
            for t in range(8):
                weights = jnp.exp2(tiles[t] * SCORE - top)
                total = total + jnp.sum(weights, axis=0, keepdims=True)
                value = keys[t][:, 192 + HEAD * h : 256 + HEAD * h]
                out = out + mm(value.T, weights.astype(BF))
            out = out / total
            os[j, HEAD * h : HEAD * h + HEAD, :] = out.astype(BF)
            stats[j, h : h + 1, :] = top + jnp.log2(total)
            stats[j, 3 + h : 4 + h, :] = jnp.sum(
                d_att.astype(F32).T * out, axis=0, keepdims=True
            )
        stats[j, 6:8, :] = jnp.zeros((2, 256), F32)
        return carry

    lax.fori_loop(0, 4, slot_step, 0)
    for j, ref in enumerate(outs):
        ref[...] = os[j]


def merged(stat_refs, out_refs):
    stats = [ref[-step % 4] for step, ref in enumerate(stat_refs)]
    rows = []
    for h in range(HEADS):
        logs = [s[h : h + 1, :] for s in stats]
        top = functools.reduce(jnp.maximum, logs)
        shares = [jnp.exp2(v - top) for v in logs]
        total = functools.reduce(jnp.add, shares)
        mixed = functools.reduce(
            jnp.add,
            [
                share * ref[HEAD * h : HEAD * h + HEAD, :].astype(F32)
                for share, ref in zip(shares, out_refs, strict=True)
            ],
        )
        rows.append(mixed / total)
    return jnp.concatenate(rows, axis=0).T.astype(BF)


def backward_kernel(tiles, first, last, unread, coords, order, *refs):
    n = len(tiles)
    refs = list(refs)

    def take(count):
        taken = refs[:count]
        del refs[:count]
        return taken

    stats = take(4 if first else 1)
    queries, keys = take(4), take(n)
    d_before = None if first else take(1)[0]
    passed = take(3 if last else 0)
    take(unread)
    if first:
        (st,) = take(1)
    else:
        (st,) = stats
    d_keys = take(n // 2)
    d_queries = take(4 if last else 1)
    ks, dks = take(2)
    dqs = take(1)[0] if last else d_queries[0]
    for i, ref in enumerate(keys):
        ks[i] = ref[...]
    dqs[...] = jnp.zeros_like(dqs) if first else d_before[...]
    for j in range(4 if first else 0):
        parts = [ref[(j - step) % 4] for step, ref in enumerate(stats)]
        logs = [p[0:3, :] for p in parts]
        top = functools.reduce(jnp.maximum, logs)
        total = functools.reduce(jnp.add, [jnp.exp2(v - top) for v in logs])
        whole = top + jnp.log2(total)
        st[j, 0:3, :] = whole
        st[j, 3:6, :] = functools.reduce(
            jnp.add, [jnp.exp2(p[0:3, :] - whole) * p[3:6, :] for p in parts]
        )
        st[j, 6:8, :] = jnp.zeros((2, 256), F32)
    gap = gap_table()

    def tile_step(i, carry):
        step = tiles[2] - tiles[0] if n > 2 else 0
        k_places = key_places(coords, order, tiles[0] + i % 2 + i // 2 * step)
        for h in range(HEADS):
            key = ks[i, :, HEAD * h : HEAD * h + HEAD]
            value = ks[i, :, 192 + HEAD * h : 256 + HEAD * h]
            key_turned = key.T
            d_key = jnp.zeros((256, HEAD), F32)
            d_value = jnp.zeros((256, HEAD), F32)
            for j in range(4):
                query = queries[j][:, HEAD * h : HEAD * h + HEAD]
                d_att = queries[j][:, 192 + HEAD * h : 256 + HEAD * h]
                scores = mask_tile(
                    mm_nt(key, query), gap, query_places(coords, order, j), k_places
                )
                weights = jnp.exp2(scores * SCORE - st[j, h : h + 1, :])
                d_weights = mm_nt(value, d_att)
                d_scores = (weights * (d_weights - st[j, 3 + h : 4 + h, :])).astype(BF)
                d_value = d_value + mm(weights.astype(BF), d_att)
                d_key = d_key + mm(d_scores, query)
                dqs[j, HEAD * h : HEAD * h + HEAD, :] += mm(key_turned, d_scores)
            dks[i, :, HEAD * h : HEAD * h + HEAD] = (d_key * SCALE).astype(BF)
            dks[i, :, 192 + HEAD * h : 256 + HEAD * h] = d_value.astype(BF)
        return carry

    lax.fori_loop(0, n, tile_step, 0)
    for i, ref in enumerate(d_keys):
        ref[...] = dks[2 * i : 2 * i + 2]
    if last:
        for j, ref in enumerate(d_queries):
            ref[0:192, :] = (dqs[j] * SCALE).astype(BF)
        for source, ref in zip(passed, d_queries[1:], strict=True):
            ref[192:384, :] = source[...]


def key_sum_kernel(own, far, near, near_too, mlp, send, kept):
    def total(a):
        parts = [ref[a].astype(F32) for ref in (own, far, near, near_too)]
        return functools.reduce(jnp.add, parts).astype(BF)

    kept[...] = total(0)
    send[0:256, :] = total(1)
    send[256:352, :] = mlp[:, 0:384]
    send[352:448, :] = mlp[:, 384:768]


def tail_kernel(
    coords, order, table, tok, cot, lna, wqkv, ga, gm, dq0, dq1, dq2, dq3, dkv0, dkv1,
    s0, s1, s2, s3, o0, wd, part, d_ln_mlp, small_in, mlp, g0, g1, g2, g3, upstream, mlp_sum, grads,
):
    outs = [o0] + [ref.at[192:384] for ref in (dq3, dq2, dq1)]
    att = merged((s0, s1, s2, s3), outs)
    upstream[256:512, :] = (mm(att, wd[...]) + part[...]).astype(BF)
    d_query = (
        dq0[...].astype(F32)
        + dq1[0:192, :].astype(F32)
        + dq2[0:192, :].astype(F32)
        + dq3[0:192, :].astype(F32)
    ).T
    d_kv = dkv0[...].astype(F32) + dkv1[0:256, :].astype(F32)
    for half in range(2):
        lanes = slice(384 * half, 384 * half + 384)
        other = dkv1[256 + 96 * half : 352 + 96 * half, :]
        mlp_sum[:, lanes] = (mlp[:, lanes].astype(F32) + other.astype(F32)).astype(BF)
    both = jnp.concatenate([d_query, d_kv[:, :192]], axis=1)
    cosine, left_sine, right_sine = spin_tables(coords, order, table)
    pieces = []
    for t in range(3):
        x = both[:, 128 * t : 128 * t + 128]
        back = (
            x * cosine
            + pltpu.roll(x * left_sine, 8, 1)
            + pltpu.roll(x * right_sine, 120, 1)
        )
        pieces += [back[:, :HEAD], back[:, HEAD:]]
    cols = []
    for h in range(HEADS):
        cols += [pieces[h], pieces[3 + h], d_kv[:, 192 + HEAD * h : 256 + HEAD * h]]
    d_joined = jnp.concatenate(cols, axis=1).astype(BF)
    turned = mm_tn(d_joined, lna[...]).astype(BF)
    for piece in range(3):
        grads[piece] = turned[192 * piece : 192 * piece + 192, :]
    grads[3] = mm_tn(att, cot[...]).astype(BF)
    for slot, ref in enumerate((g0, g1, g2, g3)):
        ref[0:192, :] = grads[(coords[2] + slot) % 4]
    d_attn = mm(d_joined, wqkv[...])
    d_mlp = d_ln_mlp[...]
    xhat, _ = normed(tok[...])
    upstream[0:256, :] = (d_attn * row(ga) + d_mlp * row(gm)).astype(BF)
    sums = [
        jnp.sum(v, axis=0, keepdims=True) for v in (d_attn * xhat, d_attn, d_mlp * xhat, d_mlp)
    ]
    bias = jnp.sum(d_joined.astype(F32), axis=0, keepdims=True)
    bias = jnp.concatenate([bias, jnp.zeros((1, 192), F32)], axis=1)
    small = jnp.concatenate([*sums, small_in[0:2, :], bias, jnp.zeros((9, 768), F32)], axis=0)
    for ref in (g0, g1, g2, g3):
        ref[192:208, :] = small.astype(BF)


def first_sum_kernel(coords, p0, p1, p2, p3, b0, b1, b2, b3, order, total):
    for slot, ref in enumerate((p0, p1, p2, p3)):
        order[(coords[2] + 4 - slot) % 4] = ref[...].astype(F32)
    rows = ((order[0] + order[1]) + (order[2] + order[3])).astype(BF)
    for block in range(4):
        total[block] = rows[48 * block : 48 * block + 48, :]
    for slot, ref in enumerate((b0, b1, b2, b3)):
        ref[0:48, :] = total[(coords[1] + slot) % 4]
        ref[48:64, :] = rows[192:208, :]


def second_sum_kernel(coords, b0, b1, b2, b3, out, order):
    for slot, ref in enumerate((b0, b1, b2, b3)):
        order[(coords[1] + 4 - slot) % 4] = ref[...].astype(F32)
    out[...] = ((order[0] + order[1]) + (order[2] + order[3])).astype(BF)


def token_kernel(tok, cot, e0, e1, b_dense, b_down, out, output):
    branch = e0[256:512, :].astype(F32) + e1[256:512, :].astype(F32)
    output[...] = (tok[...].astype(F32) + branch + row(b_dense) + row(b_down)).astype(BF)
    xhat, rstd = normed(tok[...])
    e = e0[0:256, :].astype(F32) + e1[0:256, :].astype(F32)
    inner = e - jnp.mean(e, axis=-1, keepdims=True)
    inner = inner - xhat * jnp.mean(e * xhat, axis=-1, keepdims=True)
    out[...] = (cot[...].astype(F32) + rstd * inner).astype(BF)


def quarter_kernel(coords, b0, b1, b2, b3, out):
    for slot, ref in enumerate((b0, b1, b2, b3)):
        out[(coords[1] + slot) % 4] = ref[...]


def assemble_kernel(coords, p0, p1, p2, p3, mlp, gq, gd, gu, gdn, whole):
    gu[...] = mlp[0:768, :].astype(F32)
    gdn[...] = mlp[768:1536, :].astype(F32)
    for slot, ref in enumerate((p0, p1, p2, p3)):
        whole[(coords[2] + slot) % 4] = ref[...].astype(F32)
    for block in range(12):
        gq[48 * block : 48 * block + 48, :] = whole[block // 4, block % 4]
    for block in range(4):
        gd[48 * block : 48 * block + 48, :] = whole[3, block]


def call(kernel, outs, args, scalars, scratch=(), mib=48, unread=0):
    smem = pl.BlockSpec(memory_space=pltpu.SMEM)
    vmem = pl.BlockSpec(memory_space=pltpu.VMEM)
    shapes = [jax.ShapeDtypeStruct(s, d) for s, d in outs]
    return pl.pallas_call(
        kernel,
        out_shape=shapes,
        in_specs=[smem] * scalars
        + [vmem] * (len(args) - scalars - unread)
        + [pl.BlockSpec(memory_space=pl.ANY)] * unread,
        out_specs=[vmem] * len(shapes),
        scratch_shapes=list(scratch),
        compiler_params=pltpu.CompilerParams(vmem_limit_bytes=mib << 20),
        cost_estimate=pl.CostEstimate(flops=0, bytes_accessed=1024, transcendentals=0),
    )(*args)


def hop(x, axis, step):
    n = lax.axis_size(axis)
    return lax.ppermute(x, axis, [(i, (i + step) % n) for i in range(n)])


def add(*parts):
    return functools.reduce(jnp.add, [p.astype(F32) for p in parts])


def on_device(
    tokens,
    block_order,
    cotangent,
    w_qkv,
    b_qkv,
    w_dense,
    b_dense,
    w_up,
    b_up,
    w_down,
    b_down,
    gain_attn,
    shift_attn,
    gain_mlp,
    shift_mlp,
):
    coords = jnp.stack([lax.axis_index(a) for a in CTX]).astype(jnp.int32)
    table = jnp.asarray(lane_table())
    w_turned = w_qkv.T

    qdo, kv, ln_attn, grads_mlp, small_mlp, part_mlp, d_ln_mlp = call(
        front_kernel,
        [((256, 384), BF), ((256, 384), BF), ((256, 768), BF), ((1536, 768), BF),
         ((8, 768), F32), ((256, 768), F32), ((256, 768), F32)],
        (coords, block_order, table, tokens, cotangent, w_turned, w_dense,
         gain_attn, shift_attn, gain_mlp, shift_mlp, b_qkv, w_up, b_up, w_down),
        2,
        mib=60,
    )
    grads_mlp = lax.psum_scatter(grads_mlp, ("z", "y"), scatter_dimension=0, tiled=True)
    kv_x = hop(kv, "xl", 1)
    down, up = hop(kv, "z", 1), hop(kv, "z", -1)
    down_x, up_x = hop(kv_x, "z", 1), hop(kv_x, "z", -1)
    kvs = [kv, kv_x, up, up_x, hop(down, "z", 1), hop(up_x, "z", -1), down, down_x]
    qdos = [qdo] + [hop(qdo, "y", -j) for j in (1, 2, 3)]

    *outs, stats = call(
        forward_kernel,
        [((192, 256), BF)] * 4 + [((4, 8, 256), F32)],
        (coords, block_order, *qdos, *kvs),
        2,
        scratch=[pltpu.VMEM((4, 256, 384), BF), pltpu.VMEM((4, 192, 256), BF)],
    )
    stats_all = [stats] + [hop(stats, "y", -j) for j in (1, 2, 3)]
    def backward(tiles, stats_in, before, last, after=()):
        first = before is None
        n = len(tiles)
        kept = [((4, 8, 256), F32)] if first else []
        d_out = [((192, 256), BF)] + [((384, 256), BF)] * 3 if last else [((4, 192, 256), F32)]
        scratch = [pltpu.VMEM((n, 256, 384), BF)] * 2
        if last:
            scratch.append(pltpu.VMEM((4, 192, 256), F32))
        return call(
            functools.partial(backward_kernel, tiles, first, last, len(after)),
            kept + [((2, 256, 384), BF)] * (n // 2) + d_out,
            (coords, block_order, *stats_in, *qdos, *[kvs[t] for t in tiles])
            + (() if first else (before,))
            + (tuple(outs[1:]) if last else ())
            + tuple(after),
            2,
            unread=len(after),
            scratch=scratch,
        )

    whole, d_far, d_q = backward((4, 5), stats_all, None, False)
    far = hop(d_far, "z", 2)
    d_up, d_down, d_q = backward((2, 3, 6, 7), [whole], d_q, False)
    near = [hop(d_up, "z", 1), hop(d_down, "z", -1)]
    d_kv, *d_qs = backward((0, 1), [whole], d_q, True, (far,))
    d_queries = [d_qs[0]] + [hop(d_qs[j], "y", j) for j in (1, 2, 3)]
    d_kv_send, d_kv_own = call(
        key_sum_kernel, [((448, 384), BF), ((256, 384), BF)], (d_kv, far, *near, grads_mlp), 0
    )
    d_kv_other = hop(d_kv_send, "xl", 1)
    *pieces, upstream, grads_mlp = call(
        tail_kernel,
        [((208, 768), BF)] * 4 + [((512, 768), BF), ((96, 768), BF)],
        (coords, block_order, table, tokens, cotangent, ln_attn, w_turned, gain_attn, gain_mlp,
         *d_queries, d_kv_own, d_kv_other, *stats_all, outs[0], w_dense, part_mlp,
         d_ln_mlp, small_mlp, grads_mlp),
        2,
        scratch=[pltpu.VMEM((4, 192, 768), BF)],
        mib=60,
    )
    grads_mlp = lax.all_gather(grads_mlp, ("z", "y"), axis=0, tiled=True)

    pieces = [pieces[0]] + [hop(pieces[j], "y", j) for j in (1, 2, 3)]
    upstream = add(upstream, hop(upstream, "c", 1)).astype(BF)
    upstream_far = hop(upstream, "xh", 1)
    blocks = call(
        first_sum_kernel,
        [((64, 768), BF)] * 4,
        (coords, *pieces),
        1,
        scratch=[pltpu.VMEM((4, 208, 768), F32), pltpu.VMEM((4, 48, 768), BF)],
    )
    (block,) = call(
        second_sum_kernel,
        [((64, 768), BF)],
        (coords, blocks[0], *[hop(blocks[j], "z", j) for j in (1, 2, 3)]),
        1,
        scratch=[pltpu.VMEM((4, 64, 768), F32)],
    )
    block = add(block, hop(block, "xl", 1))
    small = block[48:56]
    gains = small + hop(small, "c", 1)
    gains = gains + hop(gains, "xh", 1)
    block = block[0:48].astype(BF)
    (quarter,) = call(
        quarter_kernel,
        [((4, 48, 768), BF)],
        (coords, block, *[hop(block, "z", -j) for j in (1, 2, 3)]),
        1,
    )
    grad_turned, grad_w_dense, grad_w_up, grad_w_down = call(
        assemble_kernel,
        [((576, 768), F32), ((192, 768), F32), ((768, 768), F32), ((768, 768), F32)],
        (coords, quarter, *[hop(quarter, "y", -j) for j in (1, 2, 3)], grads_mlp),
        1,
        scratch=[pltpu.VMEM((4, 4, 48, 768), F32)],
        mib=60,
    )
    grad_tokens, output = call(
        token_kernel,
        [((256, 768), BF)] * 2,
        (tokens, cotangent, upstream, upstream_far, b_dense, b_down),
        0,
    )
    return (
        output,
        grad_tokens,
        grad_turned.T,
        small[6, :576],
        grad_w_dense,
        small[5],
        grad_w_up,
        small[4],
        grad_w_down,
        small[5],
        gains[0],
        gains[1],
        gains[2],
        gains[3],
    )


def solution(mesh):
    fine = Mesh(mesh.devices.reshape(2, 4, 4, 2, 2), CTX + TP)
    rows, cols = P(CTX, None), P(None, TP)
    return jax.shard_map(
        on_device,
        mesh=fine,
        in_specs=(
            rows, P(), rows, cols, P(TP), P(TP, None), P(), cols, P(TP), P(TP, None),
            P(), P(), P(), P(), P(),
        ),
        out_specs=(
            rows, rows, cols, P(TP), P(TP, None), P(), cols, P(TP), P(TP, None),
            P(), P(), P(), P(), P(),
        ),
        check_vma=False,
    )
```

```python
import functools
import math

import jax
import jax.numpy as jnp
import numpy as np
from jax import lax
from jax.experimental import pallas as pl
from jax.experimental.pallas import tpu as pltpu
from jax.sharding import Mesh
from jax.sharding import PartitionSpec as P

HEAD = 64
ROT = 16
HEADS = 3
EPSILON = 1e-05
MASKED = -1e30
CTX = ("xl", "z", "y")
TP = ("xh", "c")
F32 = jnp.float32
BF = jnp.bfloat16
LOG2E = math.log2(math.e)
SCALE = 1.0 / math.sqrt(HEAD)
SCORE = SCALE * LOG2E
NT = (((1,), (1,)), ((), ()))
TN = (((0,), (0,)), ((), ()))


def mm(a, b):
    return jnp.dot(a, b, preferred_element_type=F32)


def mm_nt(a, b):
    return lax.dot_general(a, b, NT, preferred_element_type=F32)


def mm_tn(a, b):
    return lax.dot_general(a, b, TN, preferred_element_type=F32)


def lane_table():
    lane = np.arange(128) % HEAD
    table = np.zeros((8, 128), np.float32)
    table[0] = np.where(lane < ROT, 10000.0 ** (-2.0 * (lane % 8) / ROT), 0.0)
    table[1] = lane < 8
    table[2] = (lane >= 8) & (lane < ROT)
    return table


def spin_tables(coords, order, table):
    shard = (coords[0] * 4 + coords[1]) * 4 + coords[2]
    step = lax.broadcasted_iota(jnp.int32, (128, 128), 0)
    places = jnp.concatenate(
        [step + order[2 * shard] * 128, step + order[2 * shard + 1] * 128], axis=0
    )
    angles = places.astype(F32) * table[0:1, :]
    sine = jnp.sin(angles)
    return jnp.cos(angles), sine * -table[1:2, :], sine * table[2:3, :]


def row(ref):
    return ref[...].reshape(1, -1)


def normed(tokens):
    values = tokens.astype(F32)
    centred = values - jnp.mean(values, axis=-1, keepdims=True)
    rstd = lax.rsqrt(jnp.mean(centred * centred, axis=-1, keepdims=True) + EPSILON)
    return centred * rstd, rstd


def front_kernel(
    coords, order, table, tok, cot, wqkv, wd, ga, sa, gm, sm, bqkv, wu, bu, wdn,
    qdo, kv, lna, gw, small, part, d_ln,
):
    xhat, _ = normed(tok[...])
    ln = (xhat * row(ga) + row(sa)).astype(BF)
    lna[...] = ln
    joined = mm_nt(ln, wqkv[...]) + row(bqkv)
    cosine, left_sine, right_sine = spin_tables(coords, order, table)
    half = lax.broadcasted_iota(jnp.int32, (256, 128), 1) < HEAD
    tiles = []
    for t in range(4):
        x = joined[:, 128 * t : 128 * t + 128]
        spun = (
            x * cosine + pltpu.roll(x, 120, 1) * left_sine + pltpu.roll(x, 8, 1) * right_sine
        )
        if t == 1:
            spun = jnp.where(half, x, spun)
        if t == 2:
            spun = jnp.where(half, spun, x)
        tiles.append(spun)
    pieces = []
    for t in range(4):
        pieces += [tiles[t][:, :HEAD], tiles[t][:, HEAD:]]
    pieces.append(joined[:, 512:576])
    d_att = mm_nt(cot[...], wd[...])
    qdo[...] = jnp.concatenate(
        [pieces[0], pieces[3], pieces[6], d_att], axis=1
    ).astype(BF)
    kv[...] = jnp.concatenate([pieces[i] for i in (1, 4, 7, 2, 5, 8)], axis=1).astype(BF)

    ln = (xhat * row(gm) + row(sm)).astype(BF)
    up = mm(ln, wu[...]) + row(bu)
    phi = 0.5 * (1.0 + lax.erf(up * math.sqrt(0.5)))
    hid = (up * phi).astype(BF)
    slope = phi + up * (jnp.exp(up * up * -0.5) * (1.0 / math.sqrt(2.0 * math.pi)))
    d_up = (mm_nt(cot[...], wdn[...]) * slope).astype(BF)
    gw[0:768, :] = mm_tn(ln, d_up).astype(BF)
    gw[768:1536, :] = mm_tn(hid, cot[...]).astype(BF)
    part[...] = mm(hid, wdn[...])
    d_ln[...] = mm_nt(d_up, wu[...])
    small[0:1, :] = jnp.sum(d_up.astype(F32), axis=0, keepdims=True)
    small[1:2, :] = jnp.sum(cot[...].astype(F32), axis=0, keepdims=True)
    small[2:8, :] = jnp.zeros((6, 768), F32)


def mask_tile(scores, gap, q_places, k_places):
    rows = []
    for kb in range(2):
        cells = []
        for qb in range(2):
            cell = scores[128 * kb : 128 * kb + 128, 128 * qb : 128 * qb + 128]
            cells.append(jnp.where(gap <= (q_places[qb] - k_places[kb]) * 128, cell, MASKED))
        rows.append(jnp.concatenate(cells, axis=1))
    return jnp.concatenate(rows, axis=0)


def gap_table():
    return lax.broadcasted_iota(jnp.int32, (128, 128), 0) - lax.broadcasted_iota(
        jnp.int32, (128, 128), 1
    )


def query_places(coords, order, slot):
    shard = (coords[0] * 4 + coords[1]) * 4 + (coords[2] + slot) % 4
    return order[2 * shard], order[2 * shard + 1]


def key_places(coords, order, tile):
    shard = ((coords[0] + tile % 2) % 2 * 4 + (coords[1] + tile // 2) % 4) * 4 + coords[2]
    return order[2 * shard], order[2 * shard + 1]


def forward_kernel(coords, order, *refs):
    queries, keys = refs[0:4], refs[4:12]
    outs, stats, qs, os = refs[12:16], refs[16], refs[17], refs[18]
    for j, ref in enumerate(queries):
        qs[j] = ref[...]
    gap = gap_table()

    def slot_step(j, carry):
        q_places = query_places(coords, order, j)
        for h in range(HEADS):
            query = qs[j, :, HEAD * h : HEAD * h + HEAD]
            d_att = qs[j, :, 192 + HEAD * h : 256 + HEAD * h]
            tiles, tops = [], []
            for t in range(8):
                key = keys[t][:, HEAD * h : HEAD * h + HEAD]
                scores = mask_tile(
                    mm_nt(key, query), gap, q_places, key_places(coords, order, t)
                )
                tiles.append(scores)
                tops.append(jnp.max(scores, axis=0, keepdims=True))
            top = functools.reduce(jnp.maximum, tops) * SCORE
            total = jnp.zeros((1, 256), F32)
            out = jnp.zeros((HEAD, 256), F32)
            for t in range(8):
                weights = jnp.exp2(tiles[t] * SCORE - top)
                total = total + jnp.sum(weights, axis=0, keepdims=True)
                value = keys[t][:, 192 + HEAD * h : 256 + HEAD * h]
                out = out + mm(value.T, weights.astype(BF))
            out = out / total
            os[j, HEAD * h : HEAD * h + HEAD, :] = out.astype(BF)
            stats[j, h : h + 1, :] = top + jnp.log2(total)
            stats[j, 3 + h : 4 + h, :] = jnp.sum(
                d_att.astype(F32).T * out, axis=0, keepdims=True
            )
        stats[j, 6:8, :] = jnp.zeros((2, 256), F32)
        return carry

    lax.fori_loop(0, 4, slot_step, 0)
    for j, ref in enumerate(outs):
        ref[...] = os[j]


def merged(stat_refs, out_refs):
    stats = [ref[-step % 4] for step, ref in enumerate(stat_refs)]
    rows = []
    for h in range(HEADS):
        logs = [s[h : h + 1, :] for s in stats]
        top = functools.reduce(jnp.maximum, logs)
        shares = [jnp.exp2(v - top) for v in logs]
        total = functools.reduce(jnp.add, shares)
        mixed = functools.reduce(
            jnp.add,
            [
                share * ref[HEAD * h : HEAD * h + HEAD, :].astype(F32)
                for share, ref in zip(shares, out_refs, strict=True)
            ],
        )
        rows.append(mixed / total)
    return jnp.concatenate(rows, axis=0).T.astype(BF)


def backward_kernel(tiles, first, last, unread, coords, order, *refs):
    n = len(tiles)
    refs = list(refs)

    def take(count):
        taken = refs[:count]
        del refs[:count]
        return taken

    stats = take(4 if first else 1)
    queries, keys = take(4), take(n)
    d_before = None if first else take(1)[0]
    passed = take(3 if last else 0)
    take(unread)
    if first:
        (st,) = take(1)
    else:
        (st,) = stats
    d_keys = take(n // 2)
    d_queries = take(4 if last else 1)
    ks, dks = take(2)
    dqs = take(1)[0] if last else d_queries[0]
    for i, ref in enumerate(keys):
        ks[i] = ref[...]
    dqs[...] = jnp.zeros_like(dqs) if first else d_before[...]
    for j in range(4 if first else 0):
        parts = [ref[(j - step) % 4] for step, ref in enumerate(stats)]
        logs = [p[0:3, :] for p in parts]
        top = functools.reduce(jnp.maximum, logs)
        total = functools.reduce(jnp.add, [jnp.exp2(v - top) for v in logs])
        whole = top + jnp.log2(total)
        st[j, 0:3, :] = whole
        st[j, 3:6, :] = functools.reduce(
            jnp.add, [jnp.exp2(p[0:3, :] - whole) * p[3:6, :] for p in parts]
        )
        st[j, 6:8, :] = jnp.zeros((2, 256), F32)
    gap = gap_table()

    def tile_step(i, carry):
        step = tiles[2] - tiles[0] if n > 2 else 0
        k_places = key_places(coords, order, tiles[0] + i % 2 + i // 2 * step)
        for h in range(HEADS):
            key = ks[i, :, HEAD * h : HEAD * h + HEAD]
            value = ks[i, :, 192 + HEAD * h : 256 + HEAD * h]
            key_turned = key.T
            d_key = jnp.zeros((256, HEAD), F32)
            d_value = jnp.zeros((256, HEAD), F32)
            for j in range(4):
                query = queries[j][:, HEAD * h : HEAD * h + HEAD]
                d_att = queries[j][:, 192 + HEAD * h : 256 + HEAD * h]
                scores = mask_tile(
                    mm_nt(key, query), gap, query_places(coords, order, j), k_places
                )
                weights = jnp.exp2(scores * SCORE - st[j, h : h + 1, :])
                d_weights = mm_nt(value, d_att)
                d_scores = (weights * (d_weights - st[j, 3 + h : 4 + h, :])).astype(BF)
                d_value = d_value + mm(weights.astype(BF), d_att)
                d_key = d_key + mm(d_scores, query)
                dqs[j, HEAD * h : HEAD * h + HEAD, :] += mm(key_turned, d_scores)
            dks[i, :, HEAD * h : HEAD * h + HEAD] = (d_key * SCALE).astype(BF)
            dks[i, :, 192 + HEAD * h : 256 + HEAD * h] = d_value.astype(BF)
        return carry

    lax.fori_loop(0, n, tile_step, 0)
    for i, ref in enumerate(d_keys):
        ref[...] = dks[2 * i : 2 * i + 2]
    if last:
        for j, ref in enumerate(d_queries):
            ref[0:192, :] = (dqs[j] * SCALE).astype(BF)
        for source, ref in zip(passed, d_queries[1:], strict=True):
            ref[192:384, :] = source[...]


def key_sum_kernel(own, far, near, near_too, send, kept):
    def total(a):
        parts = [ref[a].astype(F32) for ref in (own, far, near, near_too)]
        return functools.reduce(jnp.add, parts).astype(BF)

    kept[...] = total(0)
    send[...] = total(1)


def keep_kernel(x, after, out):
    out[...] = x[...]


def pair_kernel(x, y, after, out):
    out[...] = (x[...].astype(F32) + y[...].astype(F32)).astype(BF)


def tail_kernel(
    coords, order, table, tok, cot, lna, wqkv, ga, gm, dq0, dq1, dq2, dq3, dkv0, dkv1,
    s0, s1, s2, s3, o0, wd, part, d_ln_mlp, small_in, g0, g1, g2, g3, upstream, grads,
):
    outs = [o0] + [ref.at[192:384] for ref in (dq3, dq2, dq1)]
    att = merged((s0, s1, s2, s3), outs)
    upstream[256:512, :] = (mm(att, wd[...]) + part[...]).astype(BF)
    d_query = (
        dq0[...].astype(F32)
        + dq1[0:192, :].astype(F32)
        + dq2[0:192, :].astype(F32)
        + dq3[0:192, :].astype(F32)
    ).T
    d_kv = dkv0[...].astype(F32) + dkv1[...].astype(F32)
    both = jnp.concatenate([d_query, d_kv[:, :192]], axis=1)
    cosine, left_sine, right_sine = spin_tables(coords, order, table)
    pieces = []
    for t in range(3):
        x = both[:, 128 * t : 128 * t + 128]
        back = (
            x * cosine
            + pltpu.roll(x * left_sine, 8, 1)
            + pltpu.roll(x * right_sine, 120, 1)
        )
        pieces += [back[:, :HEAD], back[:, HEAD:]]
    cols = []
    for h in range(HEADS):
        cols += [pieces[h], pieces[3 + h], d_kv[:, 192 + HEAD * h : 256 + HEAD * h]]
    d_joined = jnp.concatenate(cols, axis=1).astype(BF)
    turned = mm_tn(d_joined, lna[...]).astype(BF)
    for piece in range(3):
        grads[piece] = turned[192 * piece : 192 * piece + 192, :]
    grads[3] = mm_tn(att, cot[...]).astype(BF)
    for slot, ref in enumerate((g0, g1, g2, g3)):
        ref[0:192, :] = grads[(coords[2] + slot) % 4]
    d_attn = mm(d_joined, wqkv[...])
    d_mlp = d_ln_mlp[...]
    xhat, _ = normed(tok[...])
    upstream[0:256, :] = (d_attn * row(ga) + d_mlp * row(gm)).astype(BF)
    sums = [
        jnp.sum(v, axis=0, keepdims=True) for v in (d_attn * xhat, d_attn, d_mlp * xhat, d_mlp)
    ]
    bias = jnp.sum(d_joined.astype(F32), axis=0, keepdims=True)
    bias = jnp.concatenate([bias, jnp.zeros((1, 192), F32)], axis=1)
    small = jnp.concatenate([*sums, small_in[0:2, :], bias, jnp.zeros((9, 768), F32)], axis=0)
    for ref in (g0, g1, g2, g3):
        ref[192:208, :] = small.astype(BF)


def first_sum_kernel(coords, p0, p1, p2, p3, b0, b1, b2, b3, order, total):
    for slot, ref in enumerate((p0, p1, p2, p3)):
        order[(coords[2] + 4 - slot) % 4] = ref[...].astype(F32)
    rows = ((order[0] + order[1]) + (order[2] + order[3])).astype(BF)
    for block in range(4):
        total[block] = rows[48 * block : 48 * block + 48, :]
    for slot, ref in enumerate((b0, b1, b2, b3)):
        ref[0:48, :] = total[(coords[1] + slot) % 4]
        ref[48:64, :] = rows[192:208, :]


def second_sum_kernel(coords, b0, b1, b2, b3, out, order):
    for slot, ref in enumerate((b0, b1, b2, b3)):
        order[(coords[1] + 4 - slot) % 4] = ref[...].astype(F32)
    out[...] = ((order[0] + order[1]) + (order[2] + order[3])).astype(BF)


def token_kernel(tok, cot, e0, e1, b_dense, b_down, out, output):
    branch = e0[256:512, :].astype(F32) + e1[256:512, :].astype(F32)
    output[...] = (tok[...].astype(F32) + branch + row(b_dense) + row(b_down)).astype(BF)
    xhat, rstd = normed(tok[...])
    e = e0[0:256, :].astype(F32) + e1[0:256, :].astype(F32)
    inner = e - jnp.mean(e, axis=-1, keepdims=True)
    inner = inner - xhat * jnp.mean(e * xhat, axis=-1, keepdims=True)
    out[...] = (cot[...].astype(F32) + rstd * inner).astype(BF)


def quarter_kernel(coords, b0, b1, b2, b3, out):
    for slot, ref in enumerate((b0, b1, b2, b3)):
        out[(coords[1] + slot) % 4] = ref[...]


def assemble_kernel(coords, p0, p1, p2, p3, mlp, gq, gd, gu, gdn, whole):
    gu[...] = mlp[0:768, :].astype(F32)
    gdn[...] = mlp[768:1536, :].astype(F32)
    for slot, ref in enumerate((p0, p1, p2, p3)):
        whole[(coords[2] + slot) % 4] = ref[...].astype(F32)
    for block in range(12):
        gq[48 * block : 48 * block + 48, :] = whole[block // 4, block % 4]
    for block in range(4):
        gd[48 * block : 48 * block + 48, :] = whole[3, block]


def call(kernel, outs, args, scalars, scratch=(), mib=48, unread=0):
    smem = pl.BlockSpec(memory_space=pltpu.SMEM)
    vmem = pl.BlockSpec(memory_space=pltpu.VMEM)
    shapes = [jax.ShapeDtypeStruct(s, d) for s, d in outs]
    return pl.pallas_call(
        kernel,
        out_shape=shapes,
        in_specs=[smem] * scalars
        + [vmem] * (len(args) - scalars - unread)
        + [pl.BlockSpec(memory_space=pl.ANY)] * unread,
        out_specs=[vmem] * len(shapes),
        scratch_shapes=list(scratch),
        compiler_params=pltpu.CompilerParams(vmem_limit_bytes=mib << 20),
        cost_estimate=pl.CostEstimate(flops=0, bytes_accessed=1024, transcendentals=0),
    )(*args)


def hop(x, axis, step):
    n = lax.axis_size(axis)
    return lax.ppermute(x, axis, [(i, (i + step) % n) for i in range(n)])


def add(*parts):
    return functools.reduce(jnp.add, [p.astype(F32) for p in parts])


def on_device(
    tokens,
    block_order,
    cotangent,
    w_qkv,
    b_qkv,
    w_dense,
    b_dense,
    w_up,
    b_up,
    w_down,
    b_down,
    gain_attn,
    shift_attn,
    gain_mlp,
    shift_mlp,
):
    coords = jnp.stack([lax.axis_index(a) for a in CTX]).astype(jnp.int32)
    table = jnp.asarray(lane_table())
    w_turned = w_qkv.T

    qdo, kv, ln_attn, grads_mlp, small_mlp, part_mlp, d_ln_mlp = call(
        front_kernel,
        [((256, 384), BF), ((256, 384), BF), ((256, 768), BF), ((1536, 768), BF),
         ((8, 768), F32), ((256, 768), F32), ((256, 768), F32)],
        (coords, block_order, table, tokens, cotangent, w_turned, w_dense,
         gain_attn, shift_attn, gain_mlp, shift_mlp, b_qkv, w_up, b_up, w_down),
        2,
        mib=60,
    )
    grads_mlp = lax.psum_scatter(grads_mlp, ("z", "y"), scatter_dimension=0, tiled=True)
    kv_x = hop(kv, "xl", 1)
    down, up = hop(kv, "z", 1), hop(kv, "z", -1)
    down_x, up_x = hop(kv_x, "z", 1), hop(kv_x, "z", -1)
    kvs = [kv, kv_x, up, up_x, hop(down, "z", 1), hop(up_x, "z", -1), down, down_x]
    qdos = [qdo] + [hop(qdo, "y", -j) for j in (1, 2, 3)]

    *outs, stats = call(
        forward_kernel,
        [((192, 256), BF)] * 4 + [((4, 8, 256), F32)],
        (coords, block_order, *qdos, *kvs),
        2,
        scratch=[pltpu.VMEM((4, 256, 384), BF), pltpu.VMEM((4, 192, 256), BF)],
    )
    stats_all = [stats] + [hop(stats, "y", -j) for j in (1, 2, 3)]
    def backward(tiles, stats_in, before, last, after=()):
        first = before is None
        n = len(tiles)
        kept = [((4, 8, 256), F32)] if first else []
        d_out = [((192, 256), BF)] + [((384, 256), BF)] * 3 if last else [((4, 192, 256), F32)]
        scratch = [pltpu.VMEM((n, 256, 384), BF)] * 2
        if last:
            scratch.append(pltpu.VMEM((4, 192, 256), F32))
        return call(
            functools.partial(backward_kernel, tiles, first, last, len(after)),
            kept + [((2, 256, 384), BF)] * (n // 2) + d_out,
            (coords, block_order, *stats_in, *qdos, *[kvs[t] for t in tiles])
            + (() if first else (before,))
            + (tuple(outs[1:]) if last else ())
            + tuple(after),
            2,
            unread=len(after),
            scratch=scratch,
        )

    whole, d_far, d_q = backward((4, 5), stats_all, None, False)
    far = hop(d_far, "z", 2)
    d_up, d_down, d_q = backward((2, 3, 6, 7), [whole], d_q, False)
    near = [hop(d_up, "z", 1), hop(d_down, "z", -1)]
    d_kv, *d_qs = backward((0, 1), [whole], d_q, True, (far,))
    d_queries = [d_qs[0]] + [hop(d_qs[j], "y", j) for j in (1, 2, 3)]
    d_kv_send, d_kv_own = call(
        key_sum_kernel, [((256, 384), BF), ((256, 384), BF)], (d_kv, far, *near), 0
    )
    d_kv_other = hop(d_kv_send, "xl", 1)
    (grads_mlp,) = call(keep_kernel, [((96, 768), BF)], (grads_mlp, d_kv_other), 0, unread=1)
    mlp_other = hop(grads_mlp, "xl", 1)
    *pieces, upstream = call(
        tail_kernel,
        [((208, 768), BF)] * 4 + [((512, 768), BF)],
        (coords, block_order, table, tokens, cotangent, ln_attn, w_turned, gain_attn, gain_mlp,
         *d_queries, d_kv_own, d_kv_other, *stats_all, outs[0], w_dense, part_mlp,
         d_ln_mlp, small_mlp),
        2,
        scratch=[pltpu.VMEM((4, 192, 768), BF)],
        mib=60,
    )
    (grads_mlp,) = call(
        pair_kernel, [((96, 768), BF)], (grads_mlp, mlp_other, upstream), 0, unread=1
    )
    grads_mlp = lax.all_gather(grads_mlp, ("z", "y"), axis=0, tiled=True)

    pieces = [pieces[0]] + [hop(pieces[j], "y", j) for j in (1, 2, 3)]
    upstream = add(upstream, hop(upstream, "c", 1)).astype(BF)
    upstream_far = hop(upstream, "xh", 1)
    blocks = call(
        first_sum_kernel,
        [((64, 768), BF)] * 4,
        (coords, *pieces),
        1,
        scratch=[pltpu.VMEM((4, 208, 768), F32), pltpu.VMEM((4, 48, 768), BF)],
    )
    (block,) = call(
        second_sum_kernel,
        [((64, 768), BF)],
        (coords, blocks[0], *[hop(blocks[j], "z", j) for j in (1, 2, 3)]),
        1,
        scratch=[pltpu.VMEM((4, 64, 768), F32)],
    )
    block = add(block, hop(block, "xl", 1))
    small = block[48:56]
    gains = small + hop(small, "c", 1)
    gains = gains + hop(gains, "xh", 1)
    block = block[0:48].astype(BF)
    (quarter,) = call(
        quarter_kernel,
        [((4, 48, 768), BF)],
        (coords, block, *[hop(block, "z", -j) for j in (1, 2, 3)]),
        1,
    )
    grad_turned, grad_w_dense, grad_w_up, grad_w_down = call(
        assemble_kernel,
        [((576, 768), F32), ((192, 768), F32), ((768, 768), F32), ((768, 768), F32)],
        (coords, quarter, *[hop(quarter, "y", -j) for j in (1, 2, 3)], grads_mlp),
        1,
        scratch=[pltpu.VMEM((4, 4, 48, 768), F32)],
        mib=60,
    )
    grad_tokens, output = call(
        token_kernel,
        [((256, 768), BF)] * 2,
        (tokens, cotangent, upstream, upstream_far, b_dense, b_down),
        0,
    )
    return (
        output,
        grad_tokens,
        grad_turned.T,
        small[6, :576],
        grad_w_dense,
        small[5],
        grad_w_up,
        small[4],
        grad_w_down,
        small[5],
        gains[0],
        gains[1],
        gains[2],
        gains[3],
    )


def solution(mesh):
    fine = Mesh(mesh.devices.reshape(2, 4, 4, 2, 2), CTX + TP)
    rows, cols = P(CTX, None), P(None, TP)
    return jax.shard_map(
        on_device,
        mesh=fine,
        in_specs=(
            rows, P(), rows, cols, P(TP), P(TP, None), P(), cols, P(TP), P(TP, None),
            P(), P(), P(), P(), P(),
        ),
        out_specs=(
            rows, rows, cols, P(TP), P(TP, None), P(), cols, P(TP), P(TP, None),
            P(), P(), P(), P(), P(),
        ),
        check_vma=False,
    )
```

```python
import functools
import math

import jax
import jax.numpy as jnp
import numpy as np
from jax import lax
from jax.experimental import pallas as pl
from jax.experimental.pallas import tpu as pltpu
from jax.sharding import Mesh
from jax.sharding import PartitionSpec as P

HEAD = 64
ROT = 16
HEADS = 3
EPSILON = 1e-05
MASKED = -1e30
CTX = ("xl", "z", "y")
TP = ("xh", "c")
F32 = jnp.float32
BF = jnp.bfloat16
LOG2E = math.log2(math.e)
SCALE = 1.0 / math.sqrt(HEAD)
SCORE = SCALE * LOG2E
NT = (((1,), (1,)), ((), ()))
TN = (((0,), (0,)), ((), ()))


def mm(a, b):
    return jnp.dot(a, b, preferred_element_type=F32)


def mm_nt(a, b):
    return lax.dot_general(a, b, NT, preferred_element_type=F32)


def mm_tn(a, b):
    return lax.dot_general(a, b, TN, preferred_element_type=F32)


def lane_table():
    lane = np.arange(128) % HEAD
    table = np.zeros((32, 256), np.float32)
    for j in range(8):
        table[j] = 10000.0 ** (-2.0 * j / ROT)
        table[8 + j, :128] = (lane == j) | (lane == j + 8)
        table[16 + j, :128] = -1.0 * (lane == j)
        table[16 + j, 128:] = lane == j + 8
    table[24, :128] = lane >= ROT
    return table


def spin_tables(coords, order, table):
    shard = (coords[0] * 4 + coords[1]) * 4 + coords[2]
    lane = lax.broadcasted_iota(jnp.int32, (8, 256), 1)
    places = lane + jnp.where(
        lane < 128, order[2 * shard] * 128, order[2 * shard + 1] * 128 - 128
    )
    angles = places.astype(F32) * table[0:8, :]

    def spread(values, lanes):
        return lax.dot_general(
            values, lanes, TN, precision=lax.Precision.HIGHEST, preferred_element_type=F32
        )

    cosine = spread(jnp.cos(angles), table[8:16, 0:128]) + table[24:25, 0:128]
    sines = spread(jnp.sin(angles), table[16:24, :])
    return cosine, sines[:, 0:128], sines[:, 128:256]


def row(ref):
    return ref[...].reshape(1, -1)


def normed(tokens):
    values = tokens.astype(F32)
    centred = values - jnp.mean(values, axis=-1, keepdims=True)
    rstd = lax.rsqrt(jnp.mean(centred * centred, axis=-1, keepdims=True) + EPSILON)
    return centred * rstd, rstd


def front_kernel(
    coords, order, table, tok, cot, wqkv, wd, ga, sa, gm, sm, bqkv, wu, bu, wdn,
    qdo, kv, lna, gw, small, part, d_ln, spin,
):
    xhat, _ = normed(tok[...])
    ln = (xhat * row(ga) + row(sa)).astype(BF)
    lna[...] = ln
    joined = mm_nt(ln, wqkv[...]) + row(bqkv)
    cosine, left_sine, right_sine = spin_tables(coords, order, table)
    for i, values in enumerate((cosine, left_sine, right_sine)):
        spin[i] = values
    half = lax.broadcasted_iota(jnp.int32, (256, 128), 1) < HEAD
    tiles = []
    for t in range(4):
        x = joined[:, 128 * t : 128 * t + 128]
        spun = (
            x * cosine + pltpu.roll(x, 120, 1) * left_sine + pltpu.roll(x, 8, 1) * right_sine
        )
        if t == 1:
            spun = jnp.where(half, x, spun)
        if t == 2:
            spun = jnp.where(half, spun, x)
        tiles.append(spun)
    pieces = []
    for t in range(4):
        pieces += [tiles[t][:, :HEAD], tiles[t][:, HEAD:]]
    pieces.append(joined[:, 512:576])
    d_att = mm_nt(cot[...], wd[...])
    qdo[...] = jnp.concatenate(
        [pieces[0], pieces[3], pieces[6], d_att], axis=1
    ).astype(BF)
    kv[...] = jnp.concatenate([pieces[i] for i in (1, 4, 7, 2, 5, 8)], axis=1).astype(BF)

    ln = (xhat * row(gm) + row(sm)).astype(BF)
    up = mm(ln, wu[...]) + row(bu)
    phi = 0.5 * (1.0 + lax.erf(up * math.sqrt(0.5)))
    hid = (up * phi).astype(BF)
    slope = phi + up * (jnp.exp(up * up * -0.5) * (1.0 / math.sqrt(2.0 * math.pi)))
    d_up = (mm_nt(cot[...], wdn[...]) * slope).astype(BF)
    gw[0:768, :] = mm_tn(ln, d_up).astype(BF)
    gw[768:1536, :] = mm_tn(hid, cot[...]).astype(BF)
    part[...] = mm(hid, wdn[...])
    d_ln[...] = mm_nt(d_up, wu[...])
    small[0:1, :] = jnp.sum(d_up.astype(F32), axis=0, keepdims=True)
    small[1:2, :] = jnp.sum(cot[...].astype(F32), axis=0, keepdims=True)
    small[2:8, :] = jnp.zeros((6, 768), F32)


def mask_tile(scores, gap, q_places, k_places):
    rows = []
    for kb in range(2):
        cells = []
        for qb in range(2):
            cell = scores[128 * kb : 128 * kb + 128, 128 * qb : 128 * qb + 128]
            cells.append(jnp.where(gap <= (q_places[qb] - k_places[kb]) * 128, cell, MASKED))
        rows.append(jnp.concatenate(cells, axis=1))
    return jnp.concatenate(rows, axis=0)


def gap_table():
    return lax.broadcasted_iota(jnp.int32, (128, 128), 0) - lax.broadcasted_iota(
        jnp.int32, (128, 128), 1
    )


def query_places(coords, order, slot):
    shard = (coords[0] * 4 + coords[1]) * 4 + (coords[2] + slot) % 4
    return order[2 * shard], order[2 * shard + 1]


def key_places(coords, order, tile):
    shard = ((coords[0] + tile % 2) % 2 * 4 + (coords[1] + tile // 2) % 4) * 4 + coords[2]
    return order[2 * shard], order[2 * shard + 1]


def forward_kernel(coords, order, *refs):
    queries, keys = refs[0:4], refs[4:12]
    outs, stats, qs, os = refs[12:16], refs[16], refs[17], refs[18]
    for j, ref in enumerate(queries):
        qs[j] = ref[...]
    gap = gap_table()

    def slot_step(j, carry):
        q_places = query_places(coords, order, j)
        for h in range(HEADS):
            query = qs[j, :, HEAD * h : HEAD * h + HEAD]
            d_att = qs[j, :, 192 + HEAD * h : 256 + HEAD * h]
            tiles, tops = [], []
            for t in range(8):
                key = keys[t][:, HEAD * h : HEAD * h + HEAD]
                scores = mask_tile(
                    mm_nt(key, query), gap, q_places, key_places(coords, order, t)
                )
                tiles.append(scores)
                tops.append(jnp.max(scores, axis=0, keepdims=True))
            top = functools.reduce(jnp.maximum, tops) * SCORE
            total = jnp.zeros((1, 256), F32)
            out = jnp.zeros((HEAD, 256), F32)
            for t in range(8):
                weights = jnp.exp2(tiles[t] * SCORE - top)
                total = total + jnp.sum(weights, axis=0, keepdims=True)
                value = keys[t][:, 192 + HEAD * h : 256 + HEAD * h]
                out = out + mm(value.T, weights.astype(BF))
            out = out / total
            os[j, HEAD * h : HEAD * h + HEAD, :] = out.astype(BF)
            stats[j, h : h + 1, :] = top + jnp.log2(total)
            stats[j, 3 + h : 4 + h, :] = jnp.sum(
                d_att.astype(F32).T * out, axis=0, keepdims=True
            )
        stats[j, 6:8, :] = jnp.zeros((2, 256), F32)
        return carry

    lax.fori_loop(0, 4, slot_step, 0)
    for j, ref in enumerate(outs):
        ref[...] = os[j]


def merged(stat_refs, out_refs):
    stats = [ref[-step % 4] for step, ref in enumerate(stat_refs)]
    rows = []
    for h in range(HEADS):
        logs = [s[h : h + 1, :] for s in stats]
        top = functools.reduce(jnp.maximum, logs)
        shares = [jnp.exp2(v - top) for v in logs]
        total = functools.reduce(jnp.add, shares)
        mixed = functools.reduce(
            jnp.add,
            [
                share * ref[HEAD * h : HEAD * h + HEAD, :].astype(F32)
                for share, ref in zip(shares, out_refs, strict=True)
            ],
        )
        rows.append(mixed / total)
    return jnp.concatenate(rows, axis=0).T.astype(BF)


def backward_kernel(tiles, first, last, unread, coords, order, *refs):
    n = len(tiles)
    refs = list(refs)

    def take(count):
        taken = refs[:count]
        del refs[:count]
        return taken

    stats = take(4 if first else 1)
    queries, keys = take(4), take(n)
    d_before = None if first else take(1)[0]
    passed = take(3 if last else 0)
    take(unread)
    if first:
        (st,) = take(1)
    else:
        (st,) = stats
    d_keys = take(n // 2)
    d_queries = take(4 if last else 1)
    ks, dks = take(2)
    dqs = take(1)[0] if last else d_queries[0]
    for i, ref in enumerate(keys):
        ks[i] = ref[...]
    dqs[...] = jnp.zeros_like(dqs) if first else d_before[...]
    for j in range(4 if first else 0):
        parts = [ref[(j - step) % 4] for step, ref in enumerate(stats)]
        logs = [p[0:3, :] for p in parts]
        top = functools.reduce(jnp.maximum, logs)
        total = functools.reduce(jnp.add, [jnp.exp2(v - top) for v in logs])
        whole = top + jnp.log2(total)
        st[j, 0:3, :] = whole
        st[j, 3:6, :] = functools.reduce(
            jnp.add, [jnp.exp2(p[0:3, :] - whole) * p[3:6, :] for p in parts]
        )
        st[j, 6:8, :] = jnp.zeros((2, 256), F32)
    gap = gap_table()

    def tile_step(i, carry):
        step = tiles[2] - tiles[0] if n > 2 else 0
        k_places = key_places(coords, order, tiles[0] + i % 2 + i // 2 * step)
        for h in range(HEADS):
            key = ks[i, :, HEAD * h : HEAD * h + HEAD]
            value = ks[i, :, 192 + HEAD * h : 256 + HEAD * h]
            key_turned = key.T
            d_key = jnp.zeros((256, HEAD), F32)
            d_value = jnp.zeros((256, HEAD), F32)
            for j in range(4):
                query = queries[j][:, HEAD * h : HEAD * h + HEAD]
                d_att = queries[j][:, 192 + HEAD * h : 256 + HEAD * h]
                scores = mask_tile(
                    mm_nt(key, query), gap, query_places(coords, order, j), k_places
                )
                weights = jnp.exp2(scores * SCORE - st[j, h : h + 1, :])
                d_weights = mm_nt(value, d_att)
                d_scores = (weights * (d_weights - st[j, 3 + h : 4 + h, :])).astype(BF)
                d_value = d_value + mm(weights.astype(BF), d_att)
                d_key = d_key + mm(d_scores, query)
                dqs[j, HEAD * h : HEAD * h + HEAD, :] += mm(key_turned, d_scores)
            dks[i, :, HEAD * h : HEAD * h + HEAD] = (d_key * SCALE).astype(BF)
            dks[i, :, 192 + HEAD * h : 256 + HEAD * h] = d_value.astype(BF)
        return carry

    lax.fori_loop(0, n, tile_step, 0)
    for i, ref in enumerate(d_keys):
        ref[...] = dks[2 * i : 2 * i + 2]
    if last:
        for j, ref in enumerate(d_queries):
            ref[0:192, :] = (dqs[j] * SCALE).astype(BF)
        for source, ref in zip(passed, d_queries[1:], strict=True):
            ref[192:384, :] = source[...]


def key_sum_kernel(own, far, near, near_too, send, kept):
    def total(a):
        parts = [ref[a].astype(F32) for ref in (own, far, near, near_too)]
        return functools.reduce(jnp.add, parts).astype(BF)

    kept[...] = total(0)
    send[...] = total(1)


def keep_kernel(x, after, out):
    out[...] = x[...]


def pair_kernel(x, y, after, out):
    out[...] = (x[...].astype(F32) + y[...].astype(F32)).astype(BF)


def tail_kernel(
    coords, tok, cot, lna, wqkv, ga, gm, spin, dq0, dq1, dq2, dq3, dkv0, dkv1,
    s0, s1, s2, s3, o0, wd, part, d_ln_mlp, small_in, g0, g1, g2, g3, upstream, grads,
):
    outs = [o0] + [ref.at[192:384] for ref in (dq3, dq2, dq1)]
    att = merged((s0, s1, s2, s3), outs)
    upstream[256:512, :] = (mm(att, wd[...]) + part[...]).astype(BF)
    d_query = (
        dq0[...].astype(F32)
        + dq1[0:192, :].astype(F32)
        + dq2[0:192, :].astype(F32)
        + dq3[0:192, :].astype(F32)
    ).T
    d_kv = dkv0[...].astype(F32) + dkv1[...].astype(F32)
    both = jnp.concatenate([d_query, d_kv[:, :192]], axis=1)
    cosine, left_sine, right_sine = spin[0], spin[1], spin[2]
    pieces = []
    for t in range(3):
        x = both[:, 128 * t : 128 * t + 128]
        back = (
            x * cosine
            + pltpu.roll(x * left_sine, 8, 1)
            + pltpu.roll(x * right_sine, 120, 1)
        )
        pieces += [back[:, :HEAD], back[:, HEAD:]]
    cols = []
    for h in range(HEADS):
        cols += [pieces[h], pieces[3 + h], d_kv[:, 192 + HEAD * h : 256 + HEAD * h]]
    d_joined = jnp.concatenate(cols, axis=1).astype(BF)
    turned = mm_tn(d_joined, lna[...]).astype(BF)
    for piece in range(3):
        grads[piece] = turned[192 * piece : 192 * piece + 192, :]
    grads[3] = mm_tn(att, cot[...]).astype(BF)
    for slot, ref in enumerate((g0, g1, g2, g3)):
        ref[0:192, :] = grads[(coords[2] + slot) % 4]
    d_attn = mm(d_joined, wqkv[...])
    d_mlp = d_ln_mlp[...]
    xhat, _ = normed(tok[...])
    upstream[0:256, :] = (d_attn * row(ga) + d_mlp * row(gm)).astype(BF)
    sums = [
        jnp.sum(v, axis=0, keepdims=True) for v in (d_attn * xhat, d_attn, d_mlp * xhat, d_mlp)
    ]
    bias = jnp.sum(d_joined.astype(F32), axis=0, keepdims=True)
    bias = jnp.concatenate([bias, jnp.zeros((1, 192), F32)], axis=1)
    small = jnp.concatenate([*sums, small_in[0:2, :], bias, jnp.zeros((9, 768), F32)], axis=0)
    for ref in (g0, g1, g2, g3):
        ref[192:208, :] = small.astype(BF)


def first_sum_kernel(coords, p0, p1, p2, p3, b0, b1, b2, b3, order, total):
    for slot, ref in enumerate((p0, p1, p2, p3)):
        order[(coords[2] + 4 - slot) % 4] = ref[...].astype(F32)
    rows = ((order[0] + order[1]) + (order[2] + order[3])).astype(BF)
    for block in range(4):
        total[block] = rows[48 * block : 48 * block + 48, :]
    for slot, ref in enumerate((b0, b1, b2, b3)):
        ref[0:48, :] = total[(coords[1] + slot) % 4]
        ref[48:64, :] = rows[192:208, :]


def second_sum_kernel(coords, b0, b1, b2, b3, out, order):
    for slot, ref in enumerate((b0, b1, b2, b3)):
        order[(coords[1] + 4 - slot) % 4] = ref[...].astype(F32)
    out[...] = ((order[0] + order[1]) + (order[2] + order[3])).astype(BF)


def token_kernel(tok, cot, e0, e1, b_dense, b_down, out, output):
    branch = e0[256:512, :].astype(F32) + e1[256:512, :].astype(F32)
    output[...] = (tok[...].astype(F32) + branch + row(b_dense) + row(b_down)).astype(BF)
    xhat, rstd = normed(tok[...])
    e = e0[0:256, :].astype(F32) + e1[0:256, :].astype(F32)
    inner = e - jnp.mean(e, axis=-1, keepdims=True)
    inner = inner - xhat * jnp.mean(e * xhat, axis=-1, keepdims=True)
    out[...] = (cot[...].astype(F32) + rstd * inner).astype(BF)


def quarter_kernel(coords, b0, b1, b2, b3, out):
    for slot, ref in enumerate((b0, b1, b2, b3)):
        out[(coords[1] + slot) % 4] = ref[...]


def assemble_kernel(coords, p0, p1, p2, p3, mlp, gq, gd, gu, gdn):
    gu[...] = mlp[0:768, :].astype(F32)
    gdn[...] = mlp[768:1536, :].astype(F32)
    for slot, ref in enumerate((p0, p1, p2, p3)):
        piece = (coords[2] + slot) % 4

        @pl.when(piece < 3)
        def _(ref=ref, piece=piece):
            for block in range(4):
                gq[piece, 48 * block : 48 * block + 48, :] = ref[block].astype(F32)

        @pl.when(piece == 3)
        def _(ref=ref):
            for block in range(4):
                gd[48 * block : 48 * block + 48, :] = ref[block].astype(F32)


def call(kernel, outs, args, scalars, scratch=(), mib=48, unread=0):
    smem = pl.BlockSpec(memory_space=pltpu.SMEM)
    vmem = pl.BlockSpec(memory_space=pltpu.VMEM)
    shapes = [jax.ShapeDtypeStruct(s, d) for s, d in outs]
    return pl.pallas_call(
        kernel,
        out_shape=shapes,
        in_specs=[smem] * scalars
        + [vmem] * (len(args) - scalars - unread)
        + [pl.BlockSpec(memory_space=pl.ANY)] * unread,
        out_specs=[vmem] * len(shapes),
        scratch_shapes=list(scratch),
        compiler_params=pltpu.CompilerParams(vmem_limit_bytes=mib << 20),
        cost_estimate=pl.CostEstimate(flops=0, bytes_accessed=1024, transcendentals=0),
    )(*args)


def hop(x, axis, step):
    n = lax.axis_size(axis)
    return lax.ppermute(x, axis, [(i, (i + step) % n) for i in range(n)])


def add(*parts):
    return functools.reduce(jnp.add, [p.astype(F32) for p in parts])


def on_device(
    tokens,
    block_order,
    cotangent,
    w_qkv,
    b_qkv,
    w_dense,
    b_dense,
    w_up,
    b_up,
    w_down,
    b_down,
    gain_attn,
    shift_attn,
    gain_mlp,
    shift_mlp,
):
    coords = jnp.stack([lax.axis_index(a) for a in CTX]).astype(jnp.int32)
    table = jnp.asarray(lane_table())
    w_turned = w_qkv.T

    qdo, kv, ln_attn, grads_mlp, small_mlp, part_mlp, d_ln_mlp, spin = call(
        front_kernel,
        [((256, 384), BF), ((256, 384), BF), ((256, 768), BF), ((1536, 768), BF),
         ((8, 768), F32), ((256, 768), F32), ((256, 768), F32), ((3, 256, 128), F32)],
        (coords, block_order, table, tokens, cotangent, w_turned, w_dense,
         gain_attn, shift_attn, gain_mlp, shift_mlp, b_qkv, w_up, b_up, w_down),
        2,
        mib=60,
    )
    grads_mlp = lax.psum_scatter(grads_mlp, ("z", "y"), scatter_dimension=0, tiled=True)
    kv_x = hop(kv, "xl", 1)
    down, up = hop(kv, "z", 1), hop(kv, "z", -1)
    down_x, up_x = hop(kv_x, "z", 1), hop(kv_x, "z", -1)
    kvs = [kv, kv_x, up, up_x, hop(down, "z", 1), hop(up_x, "z", -1), down, down_x]
    qdos = [qdo] + [hop(qdo, "y", -j) for j in (1, 2, 3)]

    *outs, stats = call(
        forward_kernel,
        [((192, 256), BF)] * 4 + [((4, 8, 256), F32)],
        (coords, block_order, *qdos, *kvs),
        2,
        scratch=[pltpu.VMEM((4, 256, 384), BF), pltpu.VMEM((4, 192, 256), BF)],
    )
    stats_all = [stats] + [hop(stats, "y", -j) for j in (1, 2, 3)]
    def backward(tiles, stats_in, before, last, after=()):
        first = before is None
        n = len(tiles)
        kept = [((4, 8, 256), F32)] if first else []
        d_out = [((192, 256), BF)] + [((384, 256), BF)] * 3 if last else [((4, 192, 256), F32)]
        scratch = [pltpu.VMEM((n, 256, 384), BF)] * 2
        if last:
            scratch.append(pltpu.VMEM((4, 192, 256), F32))
        return call(
            functools.partial(backward_kernel, tiles, first, last, len(after)),
            kept + [((2, 256, 384), BF)] * (n // 2) + d_out,
            (coords, block_order, *stats_in, *qdos, *[kvs[t] for t in tiles])
            + (() if first else (before,))
            + (tuple(outs[1:]) if last else ())
            + tuple(after),
            2,
            unread=len(after),
            scratch=scratch,
        )

    whole, d_far, d_q = backward((4, 5), stats_all, None, False)
    far = hop(d_far, "z", 2)
    d_up, d_down, d_q = backward((2, 3, 6, 7), [whole], d_q, False)
    near = [hop(d_up, "z", 1), hop(d_down, "z", -1)]
    d_kv, *d_qs = backward((0, 1), [whole], d_q, True, (far,))
    d_queries = [d_qs[0]] + [hop(d_qs[j], "y", j) for j in (1, 2, 3)]
    d_kv_send, d_kv_own = call(
        key_sum_kernel, [((256, 384), BF), ((256, 384), BF)], (d_kv, far, *near), 0
    )
    d_kv_other = hop(d_kv_send, "xl", 1)
    (grads_mlp,) = call(keep_kernel, [((96, 768), BF)], (grads_mlp, d_kv_other), 0, unread=1)
    mlp_other = hop(grads_mlp, "xl", 1)
    *pieces, upstream = call(
        tail_kernel,
        [((208, 768), BF)] * 4 + [((512, 768), BF)],
        (coords, tokens, cotangent, ln_attn, w_turned, gain_attn, gain_mlp, spin,
         *d_queries, d_kv_own, d_kv_other, *stats_all, outs[0], w_dense, part_mlp,
         d_ln_mlp, small_mlp),
        1,
        scratch=[pltpu.VMEM((4, 192, 768), BF)],
        mib=60,
    )

    pieces = [pieces[0]] + [hop(pieces[j], "y", j) for j in (1, 2, 3)]
    (grads_mlp,) = call(
        pair_kernel, [((96, 768), BF)], (grads_mlp, mlp_other, upstream), 0, unread=1
    )
    grads_mlp = lax.all_gather(grads_mlp, ("z", "y"), axis=0, tiled=True)
    upstream = add(upstream, hop(upstream, "c", 1)).astype(BF)
    upstream_far = hop(upstream, "xh", 1)
    blocks = call(
        first_sum_kernel,
        [((64, 768), BF)] * 4,
        (coords, *pieces),
        1,
        scratch=[pltpu.VMEM((4, 208, 768), F32), pltpu.VMEM((4, 48, 768), BF)],
    )
    (block,) = call(
        second_sum_kernel,
        [((64, 768), BF)],
        (coords, blocks[0], *[hop(blocks[j], "z", j) for j in (1, 2, 3)]),
        1,
        scratch=[pltpu.VMEM((4, 64, 768), F32)],
    )
    block = add(block, hop(block, "xl", 1))
    small = block[48:56]
    gains = small + hop(small, "c", 1)
    gains = gains + hop(gains, "xh", 1)
    block = block[0:48].astype(BF)
    (quarter,) = call(
        quarter_kernel,
        [((4, 48, 768), BF)],
        (coords, block, *[hop(block, "z", -j) for j in (1, 2, 3)]),
        1,
    )
    grad_turned, grad_w_dense, grad_w_up, grad_w_down = call(
        assemble_kernel,
        [((3, 192, 768), F32), ((192, 768), F32), ((768, 768), F32), ((768, 768), F32)],
        (coords, quarter, *[hop(quarter, "y", -j) for j in (1, 2, 3)], grads_mlp),
        1,
        mib=60,
    )
    grad_tokens, output = call(
        token_kernel,
        [((256, 768), BF)] * 2,
        (tokens, cotangent, upstream, upstream_far, b_dense, b_down),
        0,
    )
    return (
        output,
        grad_tokens,
        grad_turned.reshape(576, 768).T,
        small[6, :576],
        grad_w_dense,
        small[5],
        grad_w_up,
        small[4],
        grad_w_down,
        small[5],
        gains[0],
        gains[1],
        gains[2],
        gains[3],
    )


def solution(mesh):
    fine = Mesh(mesh.devices.reshape(2, 4, 4, 2, 2), CTX + TP)
    rows, cols = P(CTX, None), P(None, TP)
    return jax.shard_map(
        on_device,
        mesh=fine,
        in_specs=(
            rows, P(), rows, cols, P(TP), P(TP, None), P(), cols, P(TP), P(TP, None),
            P(), P(), P(), P(), P(),
        ),
        out_specs=(
            rows, rows, cols, P(TP), P(TP, None), P(), cols, P(TP), P(TP, None),
            P(), P(), P(), P(), P(),
        ),
        check_vma=False,
    )
```

```python
import functools
import math

import jax
import jax.numpy as jnp
import numpy as np
from jax import lax
from jax.experimental import pallas as pl
from jax.experimental.pallas import tpu as pltpu
from jax.sharding import Mesh
from jax.sharding import PartitionSpec as P

HEAD = 64
ROT = 16
HEADS = 3
EPSILON = 1e-05
MASKED = -1e30
CTX = ("xl", "z", "y")
TP = ("xh", "c")
F32 = jnp.float32
BF = jnp.bfloat16
LOG2E = math.log2(math.e)
SCALE = 1.0 / math.sqrt(HEAD)
SCORE = SCALE * LOG2E
NT = (((1,), (1,)), ((), ()))
TN = (((0,), (0,)), ((), ()))


def mm(a, b):
    return jnp.dot(a, b, preferred_element_type=F32)


def mm_nt(a, b):
    return lax.dot_general(a, b, NT, preferred_element_type=F32)


def mm_tn(a, b):
    return lax.dot_general(a, b, TN, preferred_element_type=F32)


def lane_table():
    lane = np.arange(128) % HEAD
    table = np.zeros((32, 256), np.float32)
    for j in range(8):
        table[j] = 10000.0 ** (-2.0 * j / ROT)
        table[8 + j, :128] = (lane == j) | (lane == j + 8)
        table[16 + j, :128] = -1.0 * (lane == j)
        table[16 + j, 128:] = lane == j + 8
    table[24, :128] = lane >= ROT
    return table


def spin_tables(coords, order, table):
    shard = (coords[0] * 4 + coords[1]) * 4 + coords[2]
    lane = lax.broadcasted_iota(jnp.int32, (8, 256), 1)
    places = lane + jnp.where(
        lane < 128, order[2 * shard] * 128, order[2 * shard + 1] * 128 - 128
    )
    angles = places.astype(F32) * table[0:8, :]

    def spread(values, lanes):
        return lax.dot_general(
            values, lanes, TN, precision=lax.Precision.HIGHEST, preferred_element_type=F32
        )

    cosine = spread(jnp.cos(angles), table[8:16, 0:128]) + table[24:25, 0:128]
    sines = spread(jnp.sin(angles), table[16:24, :])
    return cosine, sines[:, 0:128], sines[:, 128:256]


def row(ref):
    return ref[...].reshape(1, -1)


def normed(tokens):
    values = tokens.astype(F32)
    centred = values - jnp.mean(values, axis=-1, keepdims=True)
    rstd = lax.rsqrt(jnp.mean(centred * centred, axis=-1, keepdims=True) + EPSILON)
    return centred * rstd, rstd


def front_kernel(
    coords, order, table, tok, cot, wqkv, wd, ga, sa, gm, sm, bqkv, wu, bu, wdn,
    qdo, kv, lna, gw, small, part, d_ln, spin,
):
    xhat, _ = normed(tok[...])
    ln = (xhat * row(ga) + row(sa)).astype(BF)
    lna[...] = ln
    joined = mm_nt(ln, wqkv[...]) + row(bqkv)
    cosine, left_sine, right_sine = spin_tables(coords, order, table)
    for i, values in enumerate((cosine, left_sine, right_sine)):
        spin[i] = values
    half = lax.broadcasted_iota(jnp.int32, (256, 128), 1) < HEAD
    tiles = []
    for t in range(4):
        x = joined[:, 128 * t : 128 * t + 128]
        spun = (
            x * cosine + pltpu.roll(x, 120, 1) * left_sine + pltpu.roll(x, 8, 1) * right_sine
        )
        if t == 1:
            spun = jnp.where(half, x, spun)
        if t == 2:
            spun = jnp.where(half, spun, x)
        tiles.append(spun)
    pieces = []
    for t in range(4):
        pieces += [tiles[t][:, :HEAD], tiles[t][:, HEAD:]]
    pieces.append(joined[:, 512:576])
    d_att = mm_nt(cot[...], wd[...])
    qdo[...] = jnp.concatenate(
        [pieces[0], pieces[3], pieces[6], d_att], axis=1
    ).astype(BF)
    kv[...] = jnp.concatenate([pieces[i] for i in (1, 4, 7, 2, 5, 8)], axis=1).astype(BF)

    ln = (xhat * row(gm) + row(sm)).astype(BF)
    up = mm(ln, wu[...]) + row(bu)
    phi = 0.5 * (1.0 + lax.erf(up * math.sqrt(0.5)))
    hid = (up * phi).astype(BF)
    slope = phi + up * (jnp.exp(up * up * -0.5) * (1.0 / math.sqrt(2.0 * math.pi)))
    d_up = (mm_nt(cot[...], wdn[...]) * slope).astype(BF)
    gw[0:768, :] = mm_tn(ln, d_up).astype(BF)
    gw[768:1536, :] = mm_tn(hid, cot[...]).astype(BF)
    part[...] = mm(hid, wdn[...])
    d_ln[...] = mm_nt(d_up, wu[...])
    small[0:1, :] = jnp.sum(d_up.astype(F32), axis=0, keepdims=True)
    small[1:2, :] = jnp.sum(cot[...].astype(F32), axis=0, keepdims=True)
    small[2:8, :] = jnp.zeros((6, 768), F32)


def mask_tile(scores, gap, q_places, k_places):
    rows = []
    for kb in range(2):
        cells = []
        for qb in range(2):
            cell = scores[128 * kb : 128 * kb + 128, 128 * qb : 128 * qb + 128]
            cells.append(jnp.where(gap <= (q_places[qb] - k_places[kb]) * 128, cell, MASKED))
        rows.append(jnp.concatenate(cells, axis=1))
    return jnp.concatenate(rows, axis=0)


def gap_table():
    return lax.broadcasted_iota(jnp.int32, (128, 128), 0) - lax.broadcasted_iota(
        jnp.int32, (128, 128), 1
    )


def query_places(coords, order, slot):
    shard = (coords[0] * 4 + coords[1]) * 4 + (coords[2] + slot) % 4
    return order[2 * shard], order[2 * shard + 1]


def key_places(coords, order, tile):
    shard = ((coords[0] + tile % 2) % 2 * 4 + (coords[1] + tile // 2) % 4) * 4 + coords[2]
    return order[2 * shard], order[2 * shard + 1]


def forward_kernel(coords, order, *refs):
    queries, keys = refs[0:4], refs[4:12]
    outs, stats, qs, os = refs[12:16], refs[16], refs[17], refs[18]
    for j, ref in enumerate(queries):
        qs[j] = ref[...]
    gap = gap_table()

    def slot_step(j, carry):
        q_places = query_places(coords, order, j)
        for h in range(HEADS):
            query = qs[j, :, HEAD * h : HEAD * h + HEAD]
            d_att = qs[j, :, 192 + HEAD * h : 256 + HEAD * h]
            tiles, tops = [], []
            for t in range(8):
                key = keys[t][:, HEAD * h : HEAD * h + HEAD]
                scores = mask_tile(
                    mm_nt(key, query), gap, q_places, key_places(coords, order, t)
                )
                tiles.append(scores)
                tops.append(jnp.max(scores, axis=0, keepdims=True))
            top = functools.reduce(jnp.maximum, tops) * SCORE
            total = jnp.zeros((1, 256), F32)
            out = jnp.zeros((HEAD, 256), F32)
            for t in range(8):
                weights = jnp.exp2(tiles[t] * SCORE - top)
                total = total + jnp.sum(weights, axis=0, keepdims=True)
                value = keys[t][:, 192 + HEAD * h : 256 + HEAD * h]
                out = out + mm(value.T, weights.astype(BF))
            out = out / total
            os[j, HEAD * h : HEAD * h + HEAD, :] = out.astype(BF)
            stats[j, h : h + 1, :] = top + jnp.log2(total)
            stats[j, 3 + h : 4 + h, :] = jnp.sum(
                d_att.astype(F32).T * out, axis=0, keepdims=True
            )
        stats[j, 6:8, :] = jnp.zeros((2, 256), F32)
        return carry

    lax.fori_loop(0, 4, slot_step, 0)
    for j, ref in enumerate(outs):
        ref[...] = os[j]


def merged(stat_refs, out_refs):
    stats = [ref[-step % 4] for step, ref in enumerate(stat_refs)]
    rows = []
    for h in range(HEADS):
        logs = [s[h : h + 1, :] for s in stats]
        top = functools.reduce(jnp.maximum, logs)
        shares = [jnp.exp2(v - top) for v in logs]
        total = functools.reduce(jnp.add, shares)
        mixed = functools.reduce(
            jnp.add,
            [
                share * ref[HEAD * h : HEAD * h + HEAD, :].astype(F32)
                for share, ref in zip(shares, out_refs, strict=True)
            ],
        )
        rows.append(mixed / total)
    return jnp.concatenate(rows, axis=0).T.astype(BF)


def backward_kernel(tiles, first, last, unread, coords, order, *refs):
    n = len(tiles)
    refs = list(refs)

    def take(count):
        taken = refs[:count]
        del refs[:count]
        return taken

    stats = take(4 if first else 1)
    queries, keys = take(4), take(n)
    d_before = None if first else take(1)[0]
    passed = take(3 if last else 0)
    take(unread)
    if first:
        (st,) = take(1)
    else:
        (st,) = stats
    d_keys = take(n // 2)
    d_queries = take(4 if last else 1)
    ks, dks = take(2)
    dqs = take(1)[0] if last else d_queries[0]
    for i, ref in enumerate(keys):
        ks[i] = ref[...]
    dqs[...] = jnp.zeros_like(dqs) if first else d_before[...]
    for j in range(4 if first else 0):
        parts = [ref[(j - step) % 4] for step, ref in enumerate(stats)]
        logs = [p[0:3, :] for p in parts]
        top = functools.reduce(jnp.maximum, logs)
        total = functools.reduce(jnp.add, [jnp.exp2(v - top) for v in logs])
        whole = top + jnp.log2(total)
        st[j, 0:3, :] = whole
        st[j, 3:6, :] = functools.reduce(
            jnp.add, [jnp.exp2(p[0:3, :] - whole) * p[3:6, :] for p in parts]
        )
        st[j, 6:8, :] = jnp.zeros((2, 256), F32)
    gap = gap_table()

    def tile_step(i, carry):
        step = tiles[2] - tiles[0] if n > 2 else 0
        k_places = key_places(coords, order, tiles[0] + i % 2 + i // 2 * step)
        for h in range(HEADS):
            key = ks[i, :, HEAD * h : HEAD * h + HEAD]
            value = ks[i, :, 192 + HEAD * h : 256 + HEAD * h]
            key_turned = key.T
            d_key = jnp.zeros((256, HEAD), F32)
            d_value = jnp.zeros((256, HEAD), F32)
            for j in range(4):
                query = queries[j][:, HEAD * h : HEAD * h + HEAD]
                d_att = queries[j][:, 192 + HEAD * h : 256 + HEAD * h]
                scores = mask_tile(
                    mm_nt(key, query), gap, query_places(coords, order, j), k_places
                )
                weights = jnp.exp2(scores * SCORE - st[j, h : h + 1, :])
                d_weights = mm_nt(value, d_att)
                d_scores = (weights * (d_weights - st[j, 3 + h : 4 + h, :])).astype(BF)
                d_value = d_value + mm(weights.astype(BF), d_att)
                d_key = d_key + mm(d_scores, query)
                dqs[j, HEAD * h : HEAD * h + HEAD, :] += mm(key_turned, d_scores)
            dks[i, :, HEAD * h : HEAD * h + HEAD] = (d_key * SCALE).astype(BF)
            dks[i, :, 192 + HEAD * h : 256 + HEAD * h] = d_value.astype(BF)
        return carry

    lax.fori_loop(0, n, tile_step, 0)
    for i, ref in enumerate(d_keys):
        ref[...] = dks[2 * i : 2 * i + 2]
    if last:
        for j, ref in enumerate(d_queries):
            ref[0:192, :] = (dqs[j] * SCALE).astype(BF)
        for source, ref in zip(passed, d_queries[1:], strict=True):
            ref[192:384, :] = source[...]


def key_sum_kernel(own, far, near, near_too, send, kept):
    def total(a):
        parts = [ref[a].astype(F32) for ref in (own, far, near, near_too)]
        return functools.reduce(jnp.add, parts).astype(BF)

    kept[...] = total(0)
    send[...] = total(1)


def keep_kernel(x, after, out):
    out[...] = x[...]


def pair_kernel(x, y, after, out):
    out[...] = (x[...].astype(F32) + y[...].astype(F32)).astype(BF)


def tail_kernel(
    coords, tok, cot, lna, wqkv, ga, gm, spin, dq0, dq1, dq2, dq3, dkv0, dkv1,
    s0, s1, s2, s3, o0, wd, part, d_ln_mlp, small_in, g0, g1, g2, g3, upstream, grads,
):
    outs = [o0] + [ref.at[192:384] for ref in (dq3, dq2, dq1)]
    att = merged((s0, s1, s2, s3), outs)
    upstream[256:512, :] = (mm(att, wd[...]) + part[...]).astype(BF)
    d_query = (
        dq0[...].astype(F32)
        + dq1[0:192, :].astype(F32)
        + dq2[0:192, :].astype(F32)
        + dq3[0:192, :].astype(F32)
    ).T
    d_kv = dkv0[...].astype(F32) + dkv1[...].astype(F32)
    both = jnp.concatenate([d_query, d_kv[:, :192]], axis=1)
    cosine, left_sine, right_sine = spin[0], spin[1], spin[2]
    pieces = []
    for t in range(3):
        x = both[:, 128 * t : 128 * t + 128]
        back = (
            x * cosine
            + pltpu.roll(x * left_sine, 8, 1)
            + pltpu.roll(x * right_sine, 120, 1)
        )
        pieces += [back[:, :HEAD], back[:, HEAD:]]
    cols = []
    for h in range(HEADS):
        cols += [pieces[h], pieces[3 + h], d_kv[:, 192 + HEAD * h : 256 + HEAD * h]]
    d_joined = jnp.concatenate(cols, axis=1).astype(BF)
    turned = mm_tn(d_joined, lna[...]).astype(BF)
    for piece in range(3):
        grads[piece] = turned[192 * piece : 192 * piece + 192, :]
    grads[3] = mm_tn(att, cot[...]).astype(BF)
    for slot, ref in enumerate((g0, g1, g2, g3)):
        ref[0:192, :] = grads[(coords[2] + slot) % 4]
    d_attn = mm(d_joined, wqkv[...])
    d_mlp = d_ln_mlp[...]
    xhat, _ = normed(tok[...])
    upstream[0:256, :] = (d_attn * row(ga) + d_mlp * row(gm)).astype(BF)
    sums = [
        jnp.sum(v, axis=0, keepdims=True) for v in (d_attn * xhat, d_attn, d_mlp * xhat, d_mlp)
    ]
    bias = jnp.sum(d_joined.astype(F32), axis=0, keepdims=True)
    bias = jnp.concatenate([bias, jnp.zeros((1, 192), F32)], axis=1)
    small = jnp.concatenate([*sums, small_in[0:2, :], bias, jnp.zeros((9, 768), F32)], axis=0)
    for ref in (g0, g1, g2, g3):
        ref[192:208, :] = small.astype(BF)


def first_sum_kernel(coords, p0, p1, p2, p3, b0, b1, b2, b3, order, total):
    for slot, ref in enumerate((p0, p1, p2, p3)):
        order[(coords[2] + 4 - slot) % 4] = ref[...].astype(F32)
    rows = ((order[0] + order[1]) + (order[2] + order[3])).astype(BF)
    for block in range(4):
        total[block] = rows[48 * block : 48 * block + 48, :]
    for slot, ref in enumerate((b0, b1, b2, b3)):
        ref[0:48, :] = total[(coords[1] + slot) % 4]
        ref[48:64, :] = rows[192:208, :]


def second_sum_kernel(coords, b0, b1, b2, b3, out, order):
    for slot, ref in enumerate((b0, b1, b2, b3)):
        order[(coords[1] + 4 - slot) % 4] = ref[...].astype(F32)
    out[...] = ((order[0] + order[1]) + (order[2] + order[3])).astype(BF)


def token_kernel(tok, cot, e0, e1, b_dense, b_down, out, output):
    branch = e0[256:512, :].astype(F32) + e1[256:512, :].astype(F32)
    output[...] = (tok[...].astype(F32) + branch + row(b_dense) + row(b_down)).astype(BF)
    xhat, rstd = normed(tok[...])
    e = e0[0:256, :].astype(F32) + e1[0:256, :].astype(F32)
    inner = e - jnp.mean(e, axis=-1, keepdims=True)
    inner = inner - xhat * jnp.mean(e * xhat, axis=-1, keepdims=True)
    out[...] = (cot[...].astype(F32) + rstd * inner).astype(BF)


def quarter_kernel(coords, b0, b1, b2, b3, out):
    for slot, ref in enumerate((b0, b1, b2, b3)):
        out[(coords[1] + slot) % 4] = ref[...]


def assemble_kernel(coords, p0, p1, p2, p3, mlp, gq, gd, gu, gdn):
    step = pl.program_id(0)

    @pl.when(step < 2)
    def _():
        gu[...] = mlp[...].astype(F32)

    @pl.when(step >= 2)
    def _():
        gdn[...] = mlp[...].astype(F32)

    for slot, ref in enumerate((p0, p1, p2, p3)):
        piece = (coords[2] + slot) % 4

        @pl.when((step == 0) & (piece < 3))
        def _(ref=ref, piece=piece):
            for block in range(4):
                gq[piece, 48 * block : 48 * block + 48, :] = ref[block].astype(F32)

        @pl.when((step == 0) & (piece == 3))
        def _(ref=ref):
            for block in range(4):
                gd[48 * block : 48 * block + 48, :] = ref[block].astype(F32)


def call(kernel, outs, args, scalars, scratch=(), mib=48, unread=0):
    smem = pl.BlockSpec(memory_space=pltpu.SMEM)
    vmem = pl.BlockSpec(memory_space=pltpu.VMEM)
    shapes = [jax.ShapeDtypeStruct(s, d) for s, d in outs]
    return pl.pallas_call(
        kernel,
        out_shape=shapes,
        in_specs=[smem] * scalars
        + [vmem] * (len(args) - scalars - unread)
        + [pl.BlockSpec(memory_space=pl.ANY)] * unread,
        out_specs=[vmem] * len(shapes),
        scratch_shapes=list(scratch),
        compiler_params=pltpu.CompilerParams(vmem_limit_bytes=mib << 20),
        cost_estimate=pl.CostEstimate(flops=0, bytes_accessed=1024, transcendentals=0),
    )(*args)


def hop(x, axis, step):
    n = lax.axis_size(axis)
    return lax.ppermute(x, axis, [(i, (i + step) % n) for i in range(n)])


def add(*parts):
    return functools.reduce(jnp.add, [p.astype(F32) for p in parts])


def on_device(
    tokens,
    block_order,
    cotangent,
    w_qkv,
    b_qkv,
    w_dense,
    b_dense,
    w_up,
    b_up,
    w_down,
    b_down,
    gain_attn,
    shift_attn,
    gain_mlp,
    shift_mlp,
):
    coords = jnp.stack([lax.axis_index(a) for a in CTX]).astype(jnp.int32)
    table = jnp.asarray(lane_table())
    w_turned = w_qkv.T

    qdo, kv, ln_attn, grads_mlp, small_mlp, part_mlp, d_ln_mlp, spin = call(
        front_kernel,
        [((256, 384), BF), ((256, 384), BF), ((256, 768), BF), ((1536, 768), BF),
         ((8, 768), F32), ((256, 768), F32), ((256, 768), F32), ((3, 256, 128), F32)],
        (coords, block_order, table, tokens, cotangent, w_turned, w_dense,
         gain_attn, shift_attn, gain_mlp, shift_mlp, b_qkv, w_up, b_up, w_down),
        2,
        mib=60,
    )
    grads_mlp = lax.psum_scatter(grads_mlp, ("z", "y"), scatter_dimension=0, tiled=True)
    kv_x = hop(kv, "xl", 1)
    down, up = hop(kv, "z", 1), hop(kv, "z", -1)
    down_x, up_x = hop(kv_x, "z", 1), hop(kv_x, "z", -1)
    kvs = [kv, kv_x, up, up_x, hop(down, "z", 1), hop(up_x, "z", -1), down, down_x]
    qdos = [qdo] + [hop(qdo, "y", -j) for j in (1, 2, 3)]

    *outs, stats = call(
        forward_kernel,
        [((192, 256), BF)] * 4 + [((4, 8, 256), F32)],
        (coords, block_order, *qdos, *kvs),
        2,
        scratch=[pltpu.VMEM((4, 256, 384), BF), pltpu.VMEM((4, 192, 256), BF)],
    )
    stats_all = [stats] + [hop(stats, "y", -j) for j in (1, 2, 3)]
    def backward(tiles, stats_in, before, last, after=()):
        first = before is None
        n = len(tiles)
        kept = [((4, 8, 256), F32)] if first else []
        d_out = [((192, 256), BF)] + [((384, 256), BF)] * 3 if last else [((4, 192, 256), F32)]
        scratch = [pltpu.VMEM((n, 256, 384), BF)] * 2
        if last:
            scratch.append(pltpu.VMEM((4, 192, 256), F32))
        return call(
            functools.partial(backward_kernel, tiles, first, last, len(after)),
            kept + [((2, 256, 384), BF)] * (n // 2) + d_out,
            (coords, block_order, *stats_in, *qdos, *[kvs[t] for t in tiles])
            + (() if first else (before,))
            + (tuple(outs[1:]) if last else ())
            + tuple(after),
            2,
            unread=len(after),
            scratch=scratch,
        )

    whole, d_far, d_q = backward((4, 5), stats_all, None, False)
    far = hop(d_far, "z", 2)
    d_up, d_down, d_q = backward((2, 3, 6, 7), [whole], d_q, False)
    near = [hop(d_up, "z", 1), hop(d_down, "z", -1)]
    d_kv, *d_qs = backward((0, 1), [whole], d_q, True, (far,))
    d_queries = [d_qs[0]] + [hop(d_qs[j], "y", j) for j in (1, 2, 3)]
    d_kv_send, d_kv_own = call(
        key_sum_kernel, [((256, 384), BF), ((256, 384), BF)], (d_kv, far, *near), 0
    )
    d_kv_other = hop(d_kv_send, "xl", 1)
    (grads_mlp,) = call(keep_kernel, [((96, 768), BF)], (grads_mlp, d_kv_other), 0, unread=1)
    mlp_other = hop(grads_mlp, "xl", 1)
    *pieces, upstream = call(
        tail_kernel,
        [((208, 768), BF)] * 4 + [((512, 768), BF)],
        (coords, tokens, cotangent, ln_attn, w_turned, gain_attn, gain_mlp, spin,
         *d_queries, d_kv_own, d_kv_other, *stats_all, outs[0], w_dense, part_mlp,
         d_ln_mlp, small_mlp),
        1,
        scratch=[pltpu.VMEM((4, 192, 768), BF)],
        mib=60,
    )

    pieces = [pieces[0]] + [hop(pieces[j], "y", j) for j in (1, 2, 3)]
    (grads_mlp,) = call(
        pair_kernel, [((96, 768), BF)], (grads_mlp, mlp_other, upstream), 0, unread=1
    )
    grads_mlp = lax.all_gather(grads_mlp, ("z", "y"), axis=0, tiled=True)
    upstream = add(upstream, hop(upstream, "c", 1)).astype(BF)
    upstream_far = hop(upstream, "xh", 1)
    blocks = call(
        first_sum_kernel,
        [((64, 768), BF)] * 4,
        (coords, *pieces),
        1,
        scratch=[pltpu.VMEM((4, 208, 768), F32), pltpu.VMEM((4, 48, 768), BF)],
    )
    (block,) = call(
        second_sum_kernel,
        [((64, 768), BF)],
        (coords, blocks[0], *[hop(blocks[j], "z", j) for j in (1, 2, 3)]),
        1,
        scratch=[pltpu.VMEM((4, 64, 768), F32)],
    )
    block = add(block, hop(block, "xl", 1))
    small = block[48:56]
    gains = small + hop(small, "c", 1)
    gains = gains + hop(gains, "xh", 1)
    block = block[0:48].astype(BF)
    (quarter,) = call(
        quarter_kernel,
        [((4, 48, 768), BF)],
        (coords, block, *[hop(block, "z", -j) for j in (1, 2, 3)]),
        1,
    )
    half = (384, 768)
    piece_spec = pl.BlockSpec((4, 48, 768), lambda i: (0, 0, 0))
    grad_turned, grad_w_dense, grad_w_up, grad_w_down = pl.pallas_call(
        assemble_kernel,
        grid=(4,),
        out_shape=[
            jax.ShapeDtypeStruct(shape, F32)
            for shape in ((3, 192, 768), (192, 768), (768, 768), (768, 768))
        ],
        in_specs=[pl.BlockSpec(memory_space=pltpu.SMEM)]
        + [piece_spec] * 4
        + [pl.BlockSpec(half, lambda i: (i, 0))],
        out_specs=[
            pl.BlockSpec((3, 192, 768), lambda i: (0, 0, 0)),
            pl.BlockSpec((192, 768), lambda i: (0, 0)),
            pl.BlockSpec(half, lambda i: (jnp.minimum(i, 1), 0)),
            pl.BlockSpec(half, lambda i: (jnp.maximum(i, 2) - 2, 0)),
        ],
        compiler_params=pltpu.CompilerParams(vmem_limit_bytes=60 << 20),
        cost_estimate=pl.CostEstimate(flops=0, bytes_accessed=1024, transcendentals=0),
    )(coords, quarter, *[hop(quarter, "y", -j) for j in (1, 2, 3)], grads_mlp)
    grad_tokens, output = call(
        token_kernel,
        [((256, 768), BF)] * 2,
        (tokens, cotangent, upstream, upstream_far, b_dense, b_down),
        0,
    )
    return (
        output,
        grad_tokens,
        grad_turned.reshape(576, 768).T,
        small[6, :576],
        grad_w_dense,
        small[5],
        grad_w_up,
        small[4],
        grad_w_down,
        small[5],
        gains[0],
        gains[1],
        gains[2],
        gains[3],
    )


def solution(mesh):
    fine = Mesh(mesh.devices.reshape(2, 4, 4, 2, 2), CTX + TP)
    rows, cols = P(CTX, None), P(None, TP)
    return jax.shard_map(
        on_device,
        mesh=fine,
        in_specs=(
            rows, P(), rows, cols, P(TP), P(TP, None), P(), cols, P(TP), P(TP, None),
            P(), P(), P(), P(), P(),
        ),
        out_specs=(
            rows, rows, cols, P(TP), P(TP, None), P(), cols, P(TP), P(TP, None),
            P(), P(), P(), P(), P(),
        ),
        check_vma=False,
    )
```
